32 devices in a mesh: blk: 8 (over z, x), states: 4 (over y, core).
Axes of the slice: x: 2, y: 2, z: 4, core: 2. Of those that a mesh axis runs over, the one named last changes fastest.
Arguments:
- start_states: float32 [16, 16, 128, 512], P('blk', None, None, 'states'), may hold values from -6 to 6
- couplings: float32 [16, 128, 128], replicated, may hold values from -0.1875 to 0.1875
- potential: float32 [16, 16, 128], P('blk'), may hold values from -18 to 18
- site_offsets: int32 [16, 6, 16], P('blk'), may hold values from 0 to 15
- coupling_index: int32 [16, 7, 16], P('blk'), may hold values from 0 to 15
- degrees: int32 [512], P('states'), may hold values from 1 to 3, as said below
Outputs:
- orthonormal: float32 [16, 16, 128, 512], P('blk', 'states')
The draws below stay inside these ranges and needn't reach their ends.
Inputs may be any that keep to these rules, and one draw needn't show every extreme that they name: `degrees`: every degree from 1 to 3 belongs to some state.
All inputs are finite; a program needn't handle non-finite values.
Results may differ from the reference program's by a relative error of at most 0.0003.
Values sent between devices are 32-bit elements; how exact they have to be, the bound alone decides.
No kernel may reach another device: no remote copies, remote signals or barrier semaphores. Data moves between devices by JAX's collectives and lax.ppermute only.
A program may use at most 128 MiB of HBM per device.

```python
import jax
import jax.numpy as jnp
from jax import lax

SITES = 16
ORB = 128
S = 512
NC = 16
DEG = 3
LAYERS = 16


def draw_potential(key, part):
    layer_ids = jnp.arange(LAYERS, dtype=jnp.float32)
    amplitude = 6.0 * (1.0 + 2.0 * layer_ids / max(LAYERS - 1, 1))
    base = jax.random.uniform(key, (LAYERS, SITES, ORB), jnp.float32, minval=-1.0, maxval=1.0)
    return (amplitude[:, None, None] * base).astype(jnp.float32)


def draw_degrees(key, part):
    order = jax.random.permutation(key, S)
    return (1 + order % DEG).astype(jnp.int32)


def set_ends(entries, key, least, largest):
    place = [jax.random.randint(jax.random.fold_in(key, axis), (), 0, length) for axis, length in enumerate(entries.shape)]
    widest = entries.shape.index(max(entries.shape))
    beside = place[:widest] + [(place[widest] + 1) % entries.shape[widest]] + place[widest + 1:]
    return entries.at[tuple(place)].set(least).at[tuple(beside)].set(largest)


def levels(rng, extent, split, low, top_value):
    gain, own = 1.0, jax.random.fold_in(rng, 6)
    for position, shards_of in split:
        steps = jnp.exp(jax.random.uniform(jax.random.fold_in(own, position), (shards_of,), jnp.float32, low / len(split), top_value / len(split)))
        gain = gain * jnp.repeat(steps, extent[position] // shards_of).reshape([-1 if axis == position else 1 for axis in range(len(extent))])
    return gain


def bell_draw(rng, extent, spread, limit, cuts=(), held_as=jnp.bfloat16):
    result = spread * jax.random.normal(rng, extent, jnp.float32)
    if cuts:
        result = result * levels(rng, extent, cuts, -0.22, 0.18)
    return jnp.clip(result, -limit, limit).astype(held_as)


def setup_inputs(seed: int = 0) -> dict:
    key_list = jax.random.split(jax.random.key(seed), 7)
    return {
        "start_states": bell_draw(key_list[0], (LAYERS, SITES, ORB, S), 1.0, 6.0, ((0, 8), (3, 4)), jnp.float32),
        "couplings": bell_draw(key_list[1], (NC, ORB, ORB), (7 * ORB) ** -0.5, 0.1875, (), jnp.float32),
        "potential": draw_potential(jax.random.fold_in(key_list[6], 71), 0),
        "site_offsets": set_ends(jax.random.randint(key_list[3], (LAYERS, 6, SITES), 0, SITES), jax.random.fold_in(key_list[3], 1), 0, SITES - 1).astype(jnp.int32),
        "coupling_index": set_ends(jax.random.randint(key_list[4], (LAYERS, 7, SITES), 0, NC), jax.random.fold_in(key_list[4], 1), 0, NC - 1).astype(jnp.int32),
        "degrees": draw_degrees(jax.random.fold_in(key_list[6], 71), 0),
    }


cut_share = 0.3
exact = lax.Precision.HIGHEST

def apply_inner(padded, couplings, onsite, index_rows, offset_rows):
    middle = padded[1:-1]
    lower_layers = padded[:-2]
    upper_layers = padded[2:]
    count = onsite.shape[1]
    site_ids = jnp.arange(count, dtype=jnp.int32)
    layer_ids = jnp.arange(middle.shape[0], dtype=jnp.int32)
    summed = onsite[..., None] * middle
    for slot in range(7):
        if slot == 5:
            source = lower_layers
        elif slot == 6:
            source = upper_layers
        else:
            source = middle
        if slot == 0:
            moved = middle
        else:
            neighbour = ((site_ids[None, :] + offset_rows[:, slot - 1, :]) % count).astype(jnp.int32)
            moved = source[layer_ids[:, None], neighbour]
        blocks_used = jnp.take(couplings, index_rows[:, slot, :], axis=0)
        summed = summed + jnp.einsum('lsij,lsjn->lsin', blocks_used, moved, precision=exact)
    return summed

def reference(start_states, couplings, potential, site_offsets, coupling_index, degrees):
    row_abs = jnp.sum(jnp.abs(couplings), axis=2)
    diag_all = jnp.diagonal(couplings, axis1=1, axis2=2)
    picked_abs = row_abs[coupling_index]
    picked_diag = diag_all[coupling_index[:, 0, :]]
    centers = picked_diag + potential
    radii = picked_abs[:, 0] - jnp.abs(picked_diag) + jnp.sum(picked_abs[:, 1:], axis=1)
    upper = jnp.max(centers + radii)
    lower = jnp.min(centers - radii)
    cut_edge = lower + cut_share * (upper - lower)
    middle_value = (upper + cut_edge) / 2.0
    half_width = (upper - cut_edge) / 2.0

    def wrapped(field):
        return jnp.concatenate([field[-1:], field, field[:1]], axis=0)

    def scaled(applied, field):
        return (applied - middle_value * field) / half_width

    def apply_whole(field):
        return apply_inner(wrapped(field), couplings, potential, coupling_index, site_offsets)
    first_step = scaled(apply_whole(start_states), start_states)
    second = 2.0 * scaled(apply_whole(first_step), first_step) - start_states
    third = 2.0 * scaled(apply_whole(second), second) - first_step
    chosen = jnp.where(degrees == 1, first_step, jnp.where(degrees == 2, second, third))
    rows = chosen.reshape(-1, chosen.shape[-1])
    gram = lax.dot_general(rows.astype(jnp.float32), rows.astype(jnp.float32), (((0,), (0,)), ((), ())), precision=exact, preferred_element_type=jnp.float32)
    factor = jnp.linalg.cholesky(gram)
    identity = jnp.eye(gram.shape[0], dtype=jnp.float32)
    inverse_factor = jax.scipy.linalg.solve_triangular(factor, identity, lower=True)
    orthonormal = jnp.dot(rows.astype(jnp.float32), inverse_factor.T.astype(jnp.float32), precision=exact, preferred_element_type=jnp.float32)
    return orthonormal.reshape(chosen.shape)
```

```python
import functools

import jax
import jax.numpy as jnp
import numpy as np
from jax import lax
from jax.experimental import pallas as pl
from jax.experimental.pallas import tpu as pltpu
from jax.sharding import Mesh
from jax.sharding import PartitionSpec as P

cut_share = 0.3
exact = lax.Precision.HIGHEST
f32 = jnp.float32
bf16 = jnp.bfloat16
pivots = 4
vmem_limit = 48 * 1024 * 1024
NT = (((1,), (1,)), ((), ()))
TN = (((0,), (0,)), ((), ()))


def vmem():
    return pl.BlockSpec(memory_space=pltpu.VMEM)


def smem():
    return pl.BlockSpec(memory_space=pltpu.SMEM)


def call(body, args, specs, out_shape, scratch=(), flops=0, moved=0):
    return pl.pallas_call(
        body,
        out_shape=out_shape,
        in_specs=specs,
        out_specs=jax.tree.map(lambda _: vmem(), out_shape),
        scratch_shapes=list(scratch),
        compiler_params=pltpu.CompilerParams(vmem_limit_bytes=vmem_limit),
        cost_estimate=pl.CostEstimate(flops=flops, bytes_accessed=moved, transcendentals=0),
    )(*args)


def halves(value):
    high = value.astype(bf16)
    return high, (value - high.astype(f32)).astype(bf16)


def swap(value, axis):
    return lax.ppermute(value, axis, [(0, 1), (1, 0)])


def turn_body(x_ref, v_ref, mine_b, mine_i, other_b, other_i):
    layers, sites, _, count = v_ref.shape
    half = count // 2
    x = x_ref[0]
    for j in range(layers):
        layer = x * (layers - 1) + (1 - 2 * x) * j

        def one(s, carry):
            turned = v_ref[layer, s].T
            first, second = turned[:half], turned[half:]
            mine = jnp.where(x == 0, first, second)
            other = jnp.where(x == 0, second, first)
            if j == 0:
                mine_b[s] = mine
                other_b[s] = other
            else:
                mine_i[j - 1, s] = mine
                other_i[j - 1, s] = other
            return carry

        lax.fori_loop(0, sites, one, 0, unroll=2)


def table_body(index_ref, coup_ref, pot_ref, table_ref, ends_ref, row_abs, diag):
    entries, orb, _ = coup_ref.shape
    rows = lax.broadcasted_iota(jnp.int32, (orb, orb), 0)
    cols = lax.broadcasted_iota(jnp.int32, (orb, orb), 1)

    def entry(c, carry):
        turned = coup_ref[c].T
        high, low = halves(turned)
        table_ref[c, :, :orb] = high
        table_ref[c, :, orb:] = low
        row_abs[c] = jnp.sum(jnp.abs(turned), axis=0, keepdims=True)
        diag[c] = jnp.sum(jnp.where(rows == cols, turned, 0.0), axis=0, keepdims=True)
        return carry

    lax.fori_loop(0, entries, entry, 0)
    layers, sites, _ = pot_ref.shape
    slots = index_ref.shape[0] // (layers * sites)

    def block(r, carry):
        top, low = carry
        layer, s = r // sites, lax.rem(r, sites)
        at = layer * slots * sites + s
        own = diag[index_ref[at]]
        center = own + pot_ref[layer, pl.ds(s, 1), :]
        radius = row_abs[index_ref[at]] - jnp.abs(own)
        for k in range(1, slots):
            radius = radius + row_abs[index_ref[at + k * sites]]
        return jnp.maximum(top, center + radius), jnp.maximum(low, radius - center)

    start = jnp.full((1, orb), -jnp.inf, f32)
    top, low = lax.fori_loop(0, layers * sites, block, (start, start))
    ends_ref[...] = jnp.concatenate(
        [jnp.broadcast_to(top, (4, orb)), jnp.broadcast_to(low, (4, orb))], axis=0
    )


def step_body(order, layers_out, total, n_src, has_prev, last, *refs):
    refs = list(refs)
    take = lambda count: [refs.pop(0) for _ in range(count)]
    (source_ref, entry_ref, x_ref) = take(3)
    table_ref, pot_ref, ends_ref = take(3)
    pieces = take(n_src)
    prevs = take(has_prev)
    degree_ref = take(1)[0] if last else None
    out_ref, split = take(2)

    lookup = {}
    for piece, chain_layers in zip(pieces, order, strict=True):
        for at, layer in enumerate(chain_layers):
            lookup[layer] = (piece, at)
    sites, half, orb = pieces[0].shape[1:]
    slots = source_ref.shape[0] // (total * sites)

    top = jnp.max(ends_ref[0:1, :], axis=1, keepdims=True)
    low = -jnp.max(ends_ref[4:5, :], axis=1, keepdims=True)
    cut_edge = low + cut_share * (top - low)
    middle = (top + cut_edge) / 2.0
    gain = (1.0 if has_prev == 0 else 2.0) / ((top - cut_edge) / 2.0)

    for layer, (piece, at) in lookup.items():

        def one(s, carry):
            high, low_part = halves(piece[at, s])
            split[layer * sites + s, :half, :] = high
            split[layer * sites + s, half:, :] = low_part
            return carry

        lax.fori_loop(0, sites, one, 0, unroll=4)

    for n, layer in enumerate(layers_out):
        piece, at = lookup[layer]

        def block(s, carry):
            row = (layer - 1) * sites + s
            left = [split[source_ref[row * slots + k]] for k in range(slots)]
            right = [table_ref[entry_ref[row * slots + k]] for k in range(slots)]
            both = jnp.dot(
                jnp.concatenate(left, axis=1),
                jnp.concatenate(right, axis=0),
                preferred_element_type=f32,
            )
            applied = both[:half, :orb] + (both[:half, orb:] + both[half:, :orb])
            field = piece[at, s]
            shift = pot_ref[pl.ds(row, 1), :] - middle
            result = (applied + shift * field) * gain
            if has_prev:
                before = prevs[0][n, s]
                result = result - before
            if last:
                degree = degree_ref[...]
                result = jnp.where(degree == 1, before, jnp.where(degree == 2, field, result))
                x = x_ref[0]
                share = out_ref.shape[3]
                own = layer <= total // 2
                place = layer - 1 if own else total - layer
                place = max(place - 1, 0)
                side = x if own else 1 - x
                out_ref[side, s // share, place, lax.rem(s, share)] = result
            else:
                out_ref[n, s] = result
            return carry

        lax.fori_loop(0, sites, block, 0, unroll=2)


def step(consts, pieces, order, layers_out, total, prevs, last_shape=None, degree=None):
    source, entry, x, table, pot, ends = consts
    sites, half, orb = pieces[0].shape[1:]
    last = last_shape is not None
    shape = last_shape if last else (len(layers_out), sites, half, orb)
    args = [source, entry, x, table, pot, ends, *pieces, *prevs] + ([degree] if last else [])
    specs = [smem()] * 3 + [vmem()] * (len(args) - 3)
    return call(
        functools.partial(step_body, order, layers_out, total, len(pieces), len(prevs), last),
        args,
        specs,
        jax.ShapeDtypeStruct(shape, f32),
        [pltpu.VMEM(((total + 2) * sites, 2 * half, orb), bf16)],
        flops=2 * len(layers_out) * sites * 7 * orb * 4 * half * 2 * orb,
        moved=4 * sites * half * orb * (total + 2 + len(layers_out)),
    )


def state_order(outer, states):
    return [a * states + b for b in range(states) for a in range(outer)]


def gram_body(outer, states, *refs):
    *pieces, gram_ref, high, low = refs
    width = pieces[0].shape[4]
    col = 0
    for piece in pieces:
        _, _, layers, share, half, _ = piece.shape
        for layer in range(layers):
            for s in range(share):
                for n, src in enumerate(state_order(outer, states)):
                    part = halves(piece[src // states, src % states, layer, s])
                    at = (slice(n * half, (n + 1) * half), slice(col, col + part[0].shape[1]))
                    high[at] = part[0]
                    low[at] = part[1]
                col += part[0].shape[1]
    count = high.shape[0]
    tile = gram_ref.shape[1]
    wide = 2 * tile
    place = 0
    blocks = {}
    for i in range(0, count, wide):
        for j in range(0, i + 1, wide):
            a = [r[i : i + wide, :] for r in (high, high, low)]
            b = [r[j : j + wide, :] for r in (high, low, high)]
            blocks[i, j] = lax.dot_general(
                jnp.concatenate(a, axis=1),
                jnp.concatenate(b, axis=1),
                NT,
                preferred_element_type=f32,
            )
    for i in range(0, count, tile):
        for j in range(0, i + 1, tile):
            block = blocks[i // wide * wide, j // wide * wide]
            gram_ref[place : place + tile, :] = block[
                i % wide : i % wide + tile, j % wide : j % wide + tile
            ]
            place += tile


def rows_body(outer, states, n_pieces, *refs):
    x_ref, *pieces, high, low = refs
    x = x_ref[0]
    chain = 0
    total = sum(p.shape[2] for p in pieces)
    for piece in pieces:
        _, _, layers, share, half, orb = piece.shape
        for layer in range(layers):
            natural = x * (total - 1) + (1 - 2 * x) * chain
            for s in range(share):
                parts = [
                    piece[src // states, src % states, layer, s]
                    for src in state_order(outer, states)
                ]
                turned = jnp.concatenate(parts, axis=0).T
                a, b = halves(turned)
                high[natural, s] = a
                low[natural, s] = b
            chain += 1


def mat_mul(a, b):
    rows, inner, cols = len(a), len(b), len(b[0])
    out = []
    for i in range(rows):
        line = []
        for j in range(cols):
            total = a[i][0] * b[0][j]
            for k in range(1, inner):
                total = total + a[i][k] * b[k][j]
            line.append(total)
        out.append(line)
    return out


def flip(a):
    return [list(line) for line in zip(*a, strict=True)]


def inverse_small(a):
    size = len(a)
    if size == 1:
        return [[1.0 / a[0][0]]]
    if size == 2:
        one = 1.0 / (a[0][0] * a[1][1] - a[0][1] * a[0][1])
        off = -(a[0][1] * one)
        return [[a[1][1] * one, off], [off, a[0][0] * one]]
    h = size // 2
    corner = [line[:h] for line in a[:h]]
    side = [line[h:] for line in a[:h]]
    rest = [line[h:] for line in a[h:]]
    ci = inverse_small(corner)
    c = mat_mul(ci, side)
    update = mat_mul(flip(side), c)
    schur = [[rest[i][j] - update[i][j] for j in range(size - h)] for i in range(size - h)]
    si = inverse_small(schur)
    off = [[-v for v in line] for line in mat_mul(c, si)]
    add = mat_mul(off, flip(c))
    first = [[ci[i][j] - add[i][j] for j in range(h)] for i in range(h)]
    return [first[i] + off[i] for i in range(h)] + [
        flip(off)[i] + si[i] for i in range(size - h)
    ]


def lower_inverse_small(a):
    size = len(a)
    low = [[None] * size for _ in range(size)]
    scale = [None] * size
    for j in range(size):
        d = a[j][j]
        for k in range(j):
            d = d - low[j][k] * low[j][k]
        scale[j] = lax.rsqrt(d)
        for i in range(j + 1, size):
            v = a[i][j]
            for k in range(j):
                v = v - low[i][k] * low[j][k]
            low[i][j] = v * scale[j]
    inv = [[None] * size for _ in range(size)]
    for i in range(size):
        inv[i][i] = scale[i]
        for j in range(i):
            v = low[i][j] * inv[j][j]
            for k in range(j + 1, i):
                v = v + low[i][k] * inv[k][j]
            inv[i][j] = -(v * scale[i])
    return inv


def lower_inverse(block_ref, out_ref):
    size = block_ref.shape[0]
    lanes = lax.broadcasted_iota(jnp.int32, (8, size), 1)
    subs = lax.broadcasted_iota(jnp.int32, (8, size), 0)
    rows = [block_ref[8 * g : 8 * g + 8, :] for g in range(size // 8)]
    shape = (8, size)
    for start in range(0, size, pivots):
        group, offset = divmod(start, 8)
        inside = (lanes >= start) & (lanes < start + pivots)
        here = rows[group]
        columns = {}
        for g in range(group, size // 8):
            columns[g] = [
                jnp.broadcast_to(rows[g][:, start + k : start + k + 1], shape)
                for k in range(pivots)
            ]
        corner = [
            [
                jnp.broadcast_to(columns[group][j][offset + i : offset + i + 1, :], shape)
                for j in range(pivots)
            ]
            for i in range(pivots)
        ]
        lines = [
            jnp.where(
                inside,
                jnp.where(lanes == start + k, 1.0, 0.0),
                jnp.broadcast_to(here[offset + k : offset + k + 1, :], shape),
            )
            for k in range(pivots)
        ]
        inv = inverse_small(corner)
        weights = [functools.reduce(jnp.add, [inv[k][m] * lines[m] for m in range(pivots)]) for k in range(pivots)]
        for g in range(group, size // 8):
            change = functools.reduce(
                jnp.add, [columns[g][k] * weights[k] for k in range(pivots)]
            )
            updated = jnp.where(inside, 0.0, rows[g]) - change
            if g == group:
                updated = jnp.where(subs >= offset + pivots, updated, rows[g])
            rows[g] = updated
        low = lower_inverse_small(corner)
        for r in range(pivots):
            line = functools.reduce(jnp.add, [low[r][k] * lines[k] for k in range(r + 1)])
            rows[group] = jnp.where(subs == offset + r, line, rows[group])
    for g in range(size // 8):
        out_ref[8 * g : 8 * g + 8, :] = jnp.where(lanes <= subs + 8 * g, rows[g], 0.0)


def finish_body(gram_ref, high_ref, low_ref, out_ref, work, diag, lower, panel, inv_high, inv_low):
    size = work.shape[0]
    tile = diag.shape[0]
    place = 0
    for i in range(0, size, tile):
        for j in range(0, i + 1, tile):
            block = gram_ref[place : place + tile, :]
            place += tile
            work[i : i + tile, j : j + tile] = block
            if i != j:
                work[j : j + tile, i : i + tile] = block.T
    cols = lax.broadcasted_iota(jnp.int32, (tile, size), 1)
    local = lax.broadcasted_iota(jnp.int32, (tile, size), 0)

    def outer(b, carry):
        at = pl.multiple_of(b * tile, tile)
        diag[...] = work[pl.ds(at, tile), pl.ds(at, tile)]
        lower_inverse(diag, lower)
        inside = (cols >= at) & (cols < at + tile)
        line = jnp.where(
            inside, jnp.where(cols - at == local, 1.0, 0.0), work[pl.ds(at, tile), :]
        )
        panel[...] = jnp.dot(lower[...], line, precision=exact, preferred_element_type=f32)
        kept = jnp.where(cols < at + tile, panel[...], 0.0)
        high, low = halves(kept)
        inv_high[pl.ds(at, tile), :] = high
        inv_low[pl.ds(at, tile), :] = low

        def trailing(i, carry):
            to = pl.multiple_of(i * tile, tile)
            change = lax.dot_general(
                panel[:, pl.ds(to, tile)], panel[...], TN, precision=exact, preferred_element_type=f32
            )
            work[pl.ds(to, tile), :] = jnp.where(inside, 0.0, work[pl.ds(to, tile), :]) - change
            return carry

        lax.fori_loop(b + 1, size // tile, trailing, 0)
        return carry

    lax.fori_loop(0, size // tile, outer, 0)

    layers, share, orb, _ = out_ref.shape

    def result(r, carry):
        layer, s = r // share, lax.rem(r, share)
        a, b = high_ref[layer, s], low_ref[layer, s]
        c, d = inv_high[...], inv_low[...]
        out_ref[layer, s] = lax.dot_general(
            a, c, NT, preferred_element_type=f32
        ) + (
            lax.dot_general(a, d, NT, preferred_element_type=f32)
            + lax.dot_general(b, c, NT, preferred_element_type=f32)
        )
        return carry

    lax.fori_loop(0, layers * share, result, 0)


def group_sum(value, axis_sets):
    if not axis_sets:
        return value
    axes, *rest = axis_sets
    count = lax.axis_size(axes)
    if count == 1:
        return group_sum(value, rest)
    if count > 8 or value.shape[0] % (8 * count):
        return group_sum(lax.psum(value, axes), rest)
    me = lax.axis_index(axes)
    share = value.shape[0] // count

    def piece(k):
        return lax.dynamic_slice_in_dim(value, lax.rem(me + k, count) * share, share, axis=0)

    total = piece(0)
    got = [
        lax.ppermute(piece(k), axes, [(i, (i + k) % count) for i in range(count)])
        for k in range(1, count)
    ]
    for part in got:
        total = total + part
    total = group_sum(total, rest)
    back = [
        lax.ppermute(total, axes, [(i, (i - k) % count) for i in range(count)])
        for k in range(1, count)
    ]
    out = jnp.zeros_like(value)
    out = lax.dynamic_update_slice_in_dim(out, total, me * share, axis=0)
    for k, part in enumerate(back, 1):
        out = lax.dynamic_update_slice_in_dim(out, part, lax.rem(me + k, count) * share, axis=0)
    return out


def per_device(start_states, couplings, potential, site_offsets, coupling_index, degrees):
    layers, sites, orb, count = start_states.shape
    half = count // 2
    total = 2 * layers
    x = lax.axis_index("x").astype(jnp.int32)
    x_arr = x[None]
    depth = lax.axis_size("z")
    states_axes = ("y", "c")
    states = lax.axis_size(states_axes)
    share = sites // states

    def z_move(value, near):
        pairs = []
        for z in range(depth):
            for xx in range(2):
                d = (1 if xx else -1) * (1 if near else -1)
                pairs.append((z * 2 + xx, (z + d) % depth * 2 + xx))
        return lax.ppermute(value, ("z", "x"), pairs)

    def chained(value):
        return jnp.where(x == 1, value[::-1], value)

    with jax.named_scope("prepare"):
        mine_b, mine_i, other_b, other_i = call(
            turn_body,
            (x_arr, start_states),
            [smem(), vmem()],
            [
                jax.ShapeDtypeStruct((sites, half, orb), f32),
                jax.ShapeDtypeStruct((layers - 1, sites, half, orb), f32),
                jax.ShapeDtypeStruct((sites, half, orb), f32),
                jax.ShapeDtypeStruct((layers - 1, sites, half, orb), f32),
            ],
            moved=4 * 2 * start_states.size,
        )
        far = z_move(mine_b, True)
        partner_b = swap(other_b, "x")
        near = z_move(partner_b, False)
        partner_i = swap(other_i, "x")

        indices = jnp.concatenate([site_offsets, coupling_index], axis=1)
        lists = jnp.concatenate(
            [chained(potential), chained(jnp.swapaxes(indices, 1, 2)).astype(f32)], axis=2
        )
        their_lists = swap(lists, "x")
        table, ends = call(
            table_body,
            (coupling_index.reshape(-1), couplings, potential),
            [smem(), vmem(), vmem()],
            [
                jax.ShapeDtypeStruct((couplings.shape[0], orb, 2 * orb), bf16),
                jax.ShapeDtypeStruct((8, orb), f32),
            ],
            [pltpu.VMEM((couplings.shape[0], 1, orb), f32)] * 2,
            moved=8 * couplings.size,
        )
        ends = jnp.maximum(ends, swap(ends, "x"))
        hop = 1
        while hop < depth:
            ends = jnp.maximum(
                ends, lax.ppermute(ends, "z", [(i, (i + hop) % depth) for i in range(depth)])
            )
            hop *= 2

        chain = jnp.concatenate([lists, their_lists[::-1]], axis=0)
        pot = chain[..., :orb].reshape(total * sites, orb)
        whole = chain[..., orb:].astype(jnp.int32)
        offsets, entry = whole[..., : site_offsets.shape[1]], whole[..., site_offsets.shape[1] :]
        layer_id = jnp.arange(1, total + 1, dtype=jnp.int32)[:, None, None]
        site_id = jnp.arange(sites, dtype=jnp.int32)[None, :, None]
        slots = entry.shape[2]
        one = 1 - 2 * x
        shifts = jnp.where(
            jnp.arange(slots) == slots - 2, -one, jnp.where(jnp.arange(slots) == slots - 1, one, 0)
        ).astype(jnp.int32)
        moved = jnp.concatenate([jnp.zeros_like(offsets[..., :1]), offsets], axis=2)
        source = (layer_id + shifts) * sites + (site_id + moved) % sites
        consts = (source.reshape(-1), entry.reshape(-1), x_arr, table, pot, ends)
        degree = lax.dynamic_slice_in_dim(degrees, x * half, half)
        degree = jnp.broadcast_to(degree[:, None], (half, orb))

    outside = [1, total]
    inside = list(range(2, total))
    near, far = near[None], far[None]
    first = [mine_b[None], mine_i, partner_i[::-1], partner_b[None]]
    first_order = [[1], list(range(2, layers + 1)), list(range(layers + 1, total)), [total]]
    with jax.named_scope("first"):
        in1 = step(consts, first, first_order, inside, total, [])
        out1 = step(consts, first + [near, far], first_order + [[0], [total + 1]], outside, total, [])
    order = [outside, inside]
    ends_order = [[0], [total + 1]]
    with jax.named_scope("second"):
        far1 = z_move(out1[0], True)
        near1 = z_move(out1[1], False)
        in0 = jnp.concatenate([mine_i, partner_i[::-1]], axis=0)
        out0 = jnp.concatenate([mine_b[None], partner_b[None]], axis=0)
        in2 = step(consts, [out1, in1], order, inside, total, [in0])
        out2 = step(
            consts, [out1, in1, near1[None], far1[None]], order + ends_order, outside, total, [out0]
        )
    with jax.named_scope("third"):
        far2 = z_move(out2[0], True)
        near2 = z_move(out2[1], False)
        in3 = step(
            consts, [out2, in2], order, inside, total, [in1],
            (2, states, layers - 1, share, half, orb), degree,
        )
        group = ("x",) + states_axes

        def regroup(value):
            flat = value.reshape((2 * states,) + value.shape[2:])
            return lax.all_to_all(flat, group, 0, 0, tiled=True).reshape(value.shape)

        in3 = regroup(in3)
        out3 = step(
            consts, [out2, in2, near2[None], far2[None]], order + ends_order, outside, total, [out1],
            (2, states, 1, share, half, orb), degree,
        )
        out3 = regroup(out3)
    pieces = [out3, in3]
    width = 2 * states * half
    depth_rows = layers * share * orb
    tiles = width // orb
    with jax.named_scope("gram"):
        gram = call(
            functools.partial(gram_body, 2, states),
            pieces,
            [vmem()] * 2,
            jax.ShapeDtypeStruct((tiles * (tiles + 1) // 2 * orb, orb), f32),
            [pltpu.VMEM((width, depth_rows), bf16)] * 2,
            flops=6 * width * width * depth_rows,
            moved=4 * width * depth_rows,
        )
        high, low = call(
            functools.partial(rows_body, 2, states, 2),
            (x_arr, *pieces),
            [smem()] + [vmem()] * 2,
            [jax.ShapeDtypeStruct((layers, share, orb, width), bf16)] * 2,
            moved=8 * width * depth_rows,
        )
        gram = group_sum(gram, [("c",), ("x", "y"), ("z",)])
    with jax.named_scope("finish"):
        return call(
            finish_body,
            (gram, high, low),
            [vmem()] * 3,
            jax.ShapeDtypeStruct((layers, share, orb, width), f32),
            [
                pltpu.VMEM((width, width), f32),
                pltpu.VMEM((orb, orb), f32),
                pltpu.VMEM((orb, orb), f32),
                pltpu.VMEM((orb, width), f32),
                pltpu.VMEM((width, width), bf16),
                pltpu.VMEM((width, width), bf16),
            ],
            flops=8 * width * width * depth_rows,
            moved=8 * width * depth_rows,
        )


def solution(mesh):
    blk, states = mesh.shape["blk"], mesh.shape["states"]
    grid = Mesh(
        np.asarray(mesh.devices).reshape(blk // 2, 2, states // 2, 2), ("z", "x", "y", "c")
    )
    b, s = ("z", "x"), ("y", "c")
    in_specs = (
        P(b, None, None, s),
        P(),
        P(b, None, None),
        P(b, None, None),
        P(b, None, None),
        P(s),
    )
    return jax.shard_map(
        per_device, mesh=grid, in_specs=in_specs, out_specs=P(b, s, None, None), check_vma=False
    )
```

```python
import functools

import jax
import jax.numpy as jnp
import numpy as np
from jax import lax
from jax.experimental import pallas as pl
from jax.experimental.pallas import tpu as pltpu
from jax.sharding import Mesh
from jax.sharding import PartitionSpec as P

cut_share = 0.3
exact = lax.Precision.HIGHEST
f32 = jnp.float32
bf16 = jnp.bfloat16
pivots = 4
vmem_limit = 48 * 1024 * 1024
small = pl.CostEstimate(flops=1, bytes_accessed=1, transcendentals=0)
large = pl.CostEstimate(flops=2 * 10**11, bytes_accessed=1, transcendentals=0)
NT = (((1,), (1,)), ((), ()))
TN = (((0,), (0,)), ((), ()))


def vmem():
    return pl.BlockSpec(memory_space=pltpu.VMEM)


def smem():
    return pl.BlockSpec(memory_space=pltpu.SMEM)


def call(body, args, specs, out_shape, scratch=(), after=(), cost=small):
    skipped = len(after)

    def kernel(*refs):
        body(*refs[: len(args)], *refs[len(args) + skipped :])

    return pl.pallas_call(
        kernel,
        out_shape=out_shape,
        in_specs=[*specs, *[pl.BlockSpec(memory_space=pl.ANY)] * skipped],
        out_specs=jax.tree.map(lambda _: vmem(), out_shape),
        scratch_shapes=list(scratch),
        compiler_params=pltpu.CompilerParams(vmem_limit_bytes=vmem_limit),
        cost_estimate=cost,
    )(*args, *after)


def halves(value):
    high = value.astype(bf16)
    return high, (value - high.astype(f32)).astype(bf16)


def hold(value, *after):
    def kernel(*refs):
        pass

    return pl.pallas_call(
        kernel,
        out_shape=jax.ShapeDtypeStruct(value.shape, value.dtype),
        in_specs=[pl.BlockSpec(memory_space=pl.ANY)] * (1 + len(after)),
        out_specs=pl.BlockSpec(memory_space=pl.ANY),
        input_output_aliases={0: 0},
        cost_estimate=small,
    )(value, *after)


def swap(value, axis):
    return lax.ppermute(value, axis, [(0, 1), (1, 0)])


def turn_body(first, x_ref, v_ref, *refs):
    mine, other = refs[-2:]
    layers, sites, _, count = v_ref.shape
    half = count // 2
    x = x_ref[0]
    for j in range(mine.shape[0]):
        layer = x * (layers - 1) + (1 - 2 * x) * (first + j) if layers > 1 else 0

        def one(s, carry):
            turned = v_ref[layer, s].T
            low, high = turned[:half], turned[half:]
            mine[j, s] = jnp.where(x == 0, low, high)
            other[j, s] = jnp.where(x == 0, high, low)
            return carry

        lax.fori_loop(0, sites, one, 0, unroll=4)


def turn_first(x_arr, states):
    layers, sites, orb, count = states.shape

    def kernel(x_ref, v_ref, mine, other, mark):
        turn_body(0, x_ref, v_ref, mine, other)
        mark[...] = jnp.zeros_like(mark)

    shape = (1, sites, count // 2, orb)
    return pl.pallas_call(
        kernel,
        out_shape=[jax.ShapeDtypeStruct(shape, f32)] * 2 + [jax.ShapeDtypeStruct((8, orb), f32)],
        grid_spec=pltpu.PrefetchScalarGridSpec(
            num_scalar_prefetch=1,
            grid=(1,),
            in_specs=[
                pl.BlockSpec((1, sites, orb, count), lambda i, x: (x[0] * (layers - 1), 0, 0, 0))
            ],
            out_specs=[pl.BlockSpec(shape, lambda i, x: (0, 0, 0, 0))] * 2
            + [pl.BlockSpec((8, orb), lambda i, x: (0, 0))],
        ),
        compiler_params=pltpu.CompilerParams(vmem_limit_bytes=vmem_limit),
        cost_estimate=small,
    )(x_arr, states)


def mark_body(out_ref):
    out_ref[...] = jnp.zeros_like(out_ref)


def lists_body(x_ref, pot_ref, offset_ref, entry_ref, out_ref):
    layers, sites, _ = pot_ref.shape
    x = x_ref[0]
    out_ref[...] = jnp.zeros_like(out_ref)
    for j in range(layers):
        layer = x * (layers - 1) + (1 - 2 * x) * j
        out_ref[j, :sites, :] = pot_ref[layer]
        row = sites
        for ref in (offset_ref, entry_ref):
            out_ref[j, row : row + ref.shape[1], :sites] = ref[layer].astype(f32)
            row += 8


def table_body(index_ref, coup_ref, pot_ref, table_ref, ends_ref, row_abs, diag):
    entries, orb, _ = coup_ref.shape
    rows = lax.broadcasted_iota(jnp.int32, (orb, orb), 0)
    cols = lax.broadcasted_iota(jnp.int32, (orb, orb), 1)

    def entry(c, carry):
        turned = coup_ref[c].T
        high, low = halves(turned)
        table_ref[c, :, :orb] = high
        table_ref[c, :, orb:] = low
        row_abs[c] = jnp.sum(jnp.abs(turned), axis=0, keepdims=True)
        diag[c] = jnp.sum(jnp.where(rows == cols, turned, 0.0), axis=0, keepdims=True)
        return carry

    lax.fori_loop(0, entries, entry, 0)
    layers, sites, _ = pot_ref.shape
    slots = index_ref.shape[0] // (layers * sites)

    def block(r, carry):
        top, low = carry
        layer, s = r // sites, lax.rem(r, sites)
        at = layer * slots * sites + s
        own = diag[index_ref[at]]
        center = own + pot_ref[layer, pl.ds(s, 1), :]
        radius = row_abs[index_ref[at]] - jnp.abs(own)
        for k in range(1, slots):
            radius = radius + row_abs[index_ref[at + k * sites]]
        return jnp.maximum(top, center + radius), jnp.maximum(low, radius - center)

    start = jnp.full((1, orb), -jnp.inf, f32)
    top, low = lax.fori_loop(0, layers * sites, block, (start, start))
    ends_ref[...] = jnp.concatenate(
        [jnp.broadcast_to(top, (4, orb)), jnp.broadcast_to(low, (4, orb))], axis=0
    )


def step_body(order, layers_out, total, number, last, *refs):
    refs = list(refs)
    take = lambda count: [refs.pop(0) for _ in range(count)]
    (source_ref, entry_ref, x_ref) = take(3)
    table_ref, pot_ref = take(2)
    pieces = take(len(order))
    ends_ref = take(1)[0] if number > 1 else None
    starts = take(len(order)) if number == 2 else []
    prev = take(1)[0] if number == 3 else None
    degree_ref = take(1)[0] if last else None
    split = refs.pop()
    scaled = refs.pop() if number == 2 else None
    out_ref = refs.pop() if not last else refs[-1]

    lookup, before_of = {}, {}
    for n, chain_layers in enumerate(order):
        for at, layer in enumerate(chain_layers):
            lookup[layer] = (pieces[n], at)
            before_of[layer] = (starts[n], at) if starts else None
    sites, half, orb = pieces[0].shape[1:]
    slots = source_ref.shape[0] // (total * sites)

    if number > 1:
        top = jnp.max(ends_ref[0:1, :], axis=1, keepdims=True)
        low = -jnp.max(ends_ref[4:5, :], axis=1, keepdims=True)
        cut_edge = low + cut_share * (top - low)
        middle = (top + cut_edge) / 2.0
        gain = 1.0 / ((top - cut_edge) / 2.0)

    def field_at(layer, s):
        piece, at = lookup[layer]
        if number != 2:
            return piece[at, s]
        start, at = before_of[layer]
        return (piece[at, s] - middle * start[at, s]) * gain

    for layer in lookup:

        def one(s, carry):
            high, low_part = halves(field_at(layer, s))
            split[layer * sites + s, :half, :] = high
            split[layer * sites + s, half:, :] = low_part
            return carry

        lax.fori_loop(0, sites, one, 0, unroll=4)

    for n, layer in enumerate(layers_out):

        def block(s, carry):
            row = (layer - 1) * sites + s
            left = [split[source_ref[row * slots + k]] for k in range(slots)]
            right = [table_ref[entry_ref[row * slots + k]] for k in range(slots)]
            both = jnp.dot(
                jnp.concatenate(left, axis=1),
                jnp.concatenate(right, axis=0),
                preferred_element_type=f32,
            )
            applied = both[:half, :orb] + (both[:half, orb:] + both[half:, :orb])
            field = field_at(layer, s)
            shift = pot_ref[pl.ds(row, 1), :]
            if number == 1:
                result = applied + shift * field
            else:
                start, start_at = before_of[layer] or (prev, n)
                before = start[start_at, s]
                result = (applied + (shift - middle) * field) * (2.0 * gain) - before
            if number == 2:
                scaled[n, s] = field
            if last:
                degree = degree_ref[...]
                result = jnp.where(degree == 1, before, jnp.where(degree == 2, field, result))
                share = out_ref.shape[3]
                own = layer <= total // 2
                place = max((layer - 1 if own else total - layer) - 1, 0)
                side = (x_ref[0] if own else 1 - x_ref[0]) if out_ref.shape[0] == 2 else 0
                out_ref[side, s // share, place, lax.rem(s, share)] = result
            else:
                out_ref[n, s] = result
            return carry

        lax.fori_loop(0, sites, block, 0, unroll=4)


def step(consts, pieces, order, layers_out, total, more=(), last_shape=None, number=1, after=(), cost=small, into=None):
    sites, half, orb = pieces[0].shape[1:]
    last = last_shape is not None
    shape = last_shape if last else (len(layers_out), sites, half, orb)
    args = [*consts, *pieces, *more]
    scratch = [pltpu.VMEM(((total + 2) * sites, 2 * half, orb), bf16)]
    body = functools.partial(step_body, order, layers_out, total, number, last)
    out = jax.ShapeDtypeStruct(shape, f32)
    one_side = last and len(layers_out) == 1
    if not one_side:
        specs = [smem()] * 3 + [vmem()] * (len(args) - 3)
        return call(body, args, specs, [out, out] if number == 2 else out, scratch, after, cost)
    own = layers_out[0] == 1
    extra = [*after] + ([into] if into is not None else [])
    count = len(args)

    def kernel(*refs):
        body(*refs[:count], *refs[count + len(extra) :])

    zeros = (0,) * (len(shape) - 1)
    return pl.pallas_call(
        kernel,
        out_shape=out,
        grid_spec=pltpu.PrefetchScalarGridSpec(
            num_scalar_prefetch=3,
            grid=(1,),
            in_specs=[vmem()] * (count - 3) + [pl.BlockSpec(memory_space=pl.ANY)] * len(extra),
            out_specs=pl.BlockSpec(
                (1, *shape[1:]), lambda i, a, b, x: (x[0] if own else 1 - x[0], *zeros)
            ),
            scratch_shapes=scratch,
        ),
        input_output_aliases={count + len(after): 0} if into is not None else {},
        compiler_params=pltpu.CompilerParams(vmem_limit_bytes=vmem_limit),
        cost_estimate=cost,
    )(*args, *extra)


def all_states(edge_ref, inner_ref, chain, s):
    ref, layer = (edge_ref, 0) if chain == 0 else (inner_ref, chain - 1)
    return [ref[a, b, layer, s] for b in range(ref.shape[1]) for a in range(2)]


def gram_body(edge_ref, inner_ref, gram_ref, high, low):
    _, _, inner_layers, share, half, orb = inner_ref.shape
    col = 0
    for chain in range(inner_layers + 1):
        for s in range(share):
            for n, part in enumerate(all_states(edge_ref, inner_ref, chain, s)):
                at = (slice(n * half, (n + 1) * half), slice(col, col + orb))
                high[at], low[at] = halves(part)
            col += orb
    count = high.shape[0]
    tile = gram_ref.shape[1]
    wide = 2 * tile
    place = 0
    blocks = {}
    for i in range(0, count, wide):
        for j in range(0, i + 1, wide):
            a = [r[i : i + wide, :] for r in (high, high, low)]
            b = [r[j : j + wide, :] for r in (high, low, high)]
            blocks[i, j] = lax.dot_general(
                jnp.concatenate(a, axis=1),
                jnp.concatenate(b, axis=1),
                NT,
                preferred_element_type=f32,
            )
    for i in range(0, count, tile):
        for j in range(0, i + 1, tile):
            block = blocks[i // wide * wide, j // wide * wide]
            gram_ref[place : place + tile, :] = block[
                i % wide : i % wide + tile, j % wide : j % wide + tile
            ]
            place += tile


def rows_body(x_ref, edge_ref, inner_ref, high, low):
    x = x_ref[0]
    layers, share = high.shape[:2]
    for chain in range(layers):
        natural = x * (layers - 1) + (1 - 2 * x) * chain
        for s in range(share):
            parts = all_states(edge_ref, inner_ref, chain, s)
            a, b = halves(jnp.concatenate(parts, axis=0).T)
            high[natural, s] = a
            low[natural, s] = b


def mat_mul(a, b):
    rows, inner, cols = len(a), len(b), len(b[0])
    out = []
    for i in range(rows):
        line = []
        for j in range(cols):
            total = a[i][0] * b[0][j]
            for k in range(1, inner):
                total = total + a[i][k] * b[k][j]
            line.append(total)
        out.append(line)
    return out


def flip(a):
    return [list(line) for line in zip(*a, strict=True)]


def inverse_small(a):
    size = len(a)
    if size == 1:
        return [[1.0 / a[0][0]]]
    if size == 2:
        one = 1.0 / (a[0][0] * a[1][1] - a[0][1] * a[0][1])
        off = -(a[0][1] * one)
        return [[a[1][1] * one, off], [off, a[0][0] * one]]
    h = size // 2
    corner = [line[:h] for line in a[:h]]
    side = [line[h:] for line in a[:h]]
    rest = [line[h:] for line in a[h:]]
    ci = inverse_small(corner)
    c = mat_mul(ci, side)
    update = mat_mul(flip(side), c)
    schur = [[rest[i][j] - update[i][j] for j in range(size - h)] for i in range(size - h)]
    si = inverse_small(schur)
    off = [[-v for v in line] for line in mat_mul(c, si)]
    add = mat_mul(off, flip(c))
    first = [[ci[i][j] - add[i][j] for j in range(h)] for i in range(h)]
    return [first[i] + off[i] for i in range(h)] + [
        flip(off)[i] + si[i] for i in range(size - h)
    ]


def lower_inverse_small(a):
    size = len(a)
    low = [[None] * size for _ in range(size)]
    scale = [None] * size
    for j in range(size):
        d = a[j][j]
        for k in range(j):
            d = d - low[j][k] * low[j][k]
        scale[j] = lax.rsqrt(d)
        for i in range(j + 1, size):
            v = a[i][j]
            for k in range(j):
                v = v - low[i][k] * low[j][k]
            low[i][j] = v * scale[j]
    inv = [[None] * size for _ in range(size)]
    for i in range(size):
        inv[i][i] = scale[i]
        for j in range(i):
            v = low[i][j] * inv[j][j]
            for k in range(j + 1, i):
                v = v + low[i][k] * inv[k][j]
            inv[i][j] = -(v * scale[i])
    return inv


def lower_inverse(block_ref, out_ref):
    size = block_ref.shape[0]
    lanes = lax.broadcasted_iota(jnp.int32, (8, size), 1)
    subs = lax.broadcasted_iota(jnp.int32, (8, size), 0)
    rows = [block_ref[8 * g : 8 * g + 8, :] for g in range(size // 8)]
    shape = (8, size)
    for start in range(0, size, pivots):
        group, offset = divmod(start, 8)
        inside = (lanes >= start) & (lanes < start + pivots)
        here = rows[group]
        columns = {}
        for g in range(group, size // 8):
            columns[g] = [
                jnp.broadcast_to(rows[g][:, start + k : start + k + 1], shape)
                for k in range(pivots)
            ]
        corner = [
            [
                jnp.broadcast_to(columns[group][j][offset + i : offset + i + 1, :], shape)
                for j in range(pivots)
            ]
            for i in range(pivots)
        ]
        lines = [
            jnp.where(
                inside,
                jnp.where(lanes == start + k, 1.0, 0.0),
                jnp.broadcast_to(here[offset + k : offset + k + 1, :], shape),
            )
            for k in range(pivots)
        ]
        inv = inverse_small(corner)
        weights = [functools.reduce(jnp.add, [inv[k][m] * lines[m] for m in range(pivots)]) for k in range(pivots)]
        for g in range(group, size // 8):
            change = functools.reduce(
                jnp.add, [columns[g][k] * weights[k] for k in range(pivots)]
            )
            updated = jnp.where(inside, 0.0, rows[g]) - change
            if g == group:
                updated = jnp.where(subs >= offset + pivots, updated, rows[g])
            rows[g] = updated
        low = lower_inverse_small(corner)
        for r in range(pivots):
            line = functools.reduce(jnp.add, [low[r][k] * lines[k] for k in range(r + 1)])
            rows[group] = jnp.where(subs == offset + r, line, rows[group])
    for g in range(size // 8):
        out_ref[8 * g : 8 * g + 8, :] = jnp.where(lanes <= subs + 8 * g, rows[g], 0.0)


def three(left, right):
    a, b = halves(left)
    c, d = halves(right)
    return jnp.dot(
        jnp.concatenate([a, a, b], axis=1),
        jnp.concatenate([c, d, c], axis=0),
        preferred_element_type=f32,
    )


def finish_body(gram_ref, high_ref, low_ref, out_ref, work, diag, lower, panel, inv):
    size = work.shape[0]
    tile = diag.shape[0]
    place = 0
    for i in range(0, size, tile):
        for j in range(0, i + 1, tile):
            block = gram_ref[place : place + tile, :]
            place += tile
            work[i : i + tile, j : j + tile] = block
            if i != j:
                work[j : j + tile, i : i + tile] = block.T
    cols = lax.broadcasted_iota(jnp.int32, (tile, size), 1)
    local = lax.broadcasted_iota(jnp.int32, (tile, size), 0)

    def outer(b, carry):
        at = pl.multiple_of(b * tile, tile)
        diag[...] = work[pl.ds(at, tile), pl.ds(at, tile)]
        lower_inverse(diag, lower)
        inside = (cols >= at) & (cols < at + tile)
        line = jnp.where(
            inside, jnp.where(cols - at == local, 1.0, 0.0), work[pl.ds(at, tile), :]
        )
        panel[...] = three(lower[...], line)
        kept = jnp.where(cols < at + tile, panel[...], 0.0)
        high, low = halves(kept)
        inv[pl.ds(at, tile), :size] = high
        inv[pl.ds(at, tile), size:] = low

        def trailing(i, carry):
            to = pl.multiple_of(i * tile, tile)
            change = three(panel[:, pl.ds(to, tile)].T, panel[...])
            work[pl.ds(to, tile), :] = jnp.where(inside, 0.0, work[pl.ds(to, tile), :]) - change
            return carry

        lax.fori_loop(b + 1, size // tile, trailing, 0)
        return carry

    lax.fori_loop(0, size // tile, outer, 0)

    layers, share, orb, _ = out_ref.shape

    def result(s, carry):
        a = jnp.concatenate([high_ref[n, s] for n in range(layers)], axis=0)
        b = jnp.concatenate([low_ref[n, s] for n in range(layers)], axis=0)
        for first in range(0, size, 2 * tile):
            last = first + 2 * tile
            c = inv[first:last, :last]
            d = inv[first:last, size : size + last]
            total = lax.dot_general(
                jnp.concatenate([a[:, :last], a[:, :last], b[:, :last]], axis=1),
                jnp.concatenate([c, d, c], axis=1),
                NT,
                preferred_element_type=f32,
            )
            for n in range(layers):
                out_ref[n, s, :, first:last] = total[n * orb : (n + 1) * orb]
        return carry

    lax.fori_loop(0, share, result, 0)


def group_sum(value, axis_sets):
    if not axis_sets:
        return value
    axes, *rest = axis_sets
    count = lax.axis_size(axes)
    if count == 1:
        return group_sum(value, rest)
    if not rest and count & (count - 1) == 0:
        hop = 1
        while hop < count:
            value = value + lax.ppermute(value, axes, [(i, i ^ hop) for i in range(count)])
            hop *= 2
        return value
    if count > 8 or value.shape[0] % (8 * count):
        return group_sum(lax.psum(value, axes), rest)
    me = lax.axis_index(axes)
    share = value.shape[0] // count

    def piece(k):
        return lax.dynamic_slice_in_dim(value, lax.rem(me + k, count) * share, share, axis=0)

    total = piece(0)
    got = [
        lax.ppermute(piece(k), axes, [(i, (i + k) % count) for i in range(count)])
        for k in range(1, count)
    ]
    for part in got:
        total = total + part
    total = group_sum(total, rest)
    back = [
        lax.ppermute(total, axes, [(i, (i - k) % count) for i in range(count)])
        for k in range(1, count)
    ]
    out = jnp.zeros_like(value)
    out = lax.dynamic_update_slice_in_dim(out, total, me * share, axis=0)
    for k, part in enumerate(back, 1):
        out = lax.dynamic_update_slice_in_dim(out, part, lax.rem(me + k, count) * share, axis=0)
    return out


def per_device(start_states, couplings, potential, site_offsets, coupling_index, degrees):
    layers, sites, orb, count = start_states.shape
    half = count // 2
    total = 2 * layers
    x = lax.axis_index("x").astype(jnp.int32)
    x_arr = x[None]
    depth = lax.axis_size("z")
    states_axes = ("y", "c")
    states = lax.axis_size(states_axes)
    share = sites // states

    def z_move(value, near):
        pairs = []
        for z in range(depth):
            for xx in range(2):
                d = (1 if xx else -1) * (1 if near else -1)
                pairs.append((z * 2 + xx, (z + d) % depth * 2 + xx))
        return lax.ppermute(value, ("z", "x"), pairs)

    with jax.named_scope("prepare"):
        mine_b, other_b, mark = turn_first(x_arr, start_states)
        far = z_move(mine_b, True)
        partner_b = swap(other_b, "x")
        mark = swap(mark, "c")
        lists = call(
            lists_body,
            (x_arr, potential, site_offsets, coupling_index),
            [smem(), vmem(), vmem(), vmem()],
            jax.ShapeDtypeStruct((layers, sites + 16, orb), f32),
            after=(mine_b,),
        )
        their_lists = swap(lists, "x")
        mine_i, other_i = call(
            functools.partial(turn_body, 1),
            (x_arr, start_states),
            [smem(), vmem()],
            [jax.ShapeDtypeStruct((layers - 1, sites, half, orb), f32)] * 2,
            after=(mine_b,),
        )
        table, ends = call(
            table_body,
            (coupling_index.reshape(-1), couplings, potential),
            [smem(), vmem(), vmem()],
            [
                jax.ShapeDtypeStruct((couplings.shape[0], orb, 2 * orb), bf16),
                jax.ShapeDtypeStruct((8, orb), f32),
            ],
            [pltpu.VMEM((couplings.shape[0], 1, orb), f32)] * 2,
            after=(mark,),
        )
        partner_b = hold(partner_b, far, table)
        devices = 2 * depth
        ends = jnp.broadcast_to(ends[None], (devices, *ends.shape))
        ends = jnp.max(lax.all_to_all(ends, ("z", "x"), 0, 0, tiled=True), axis=0)
        near = z_move(partner_b, False)
        partner_i = swap(hold(other_i, partner_b), "x")
        chain = jnp.concatenate([lists, their_lists[::-1]], axis=0)
        pot = chain[:, :sites].reshape(total * sites, orb)
        whole = jnp.swapaxes(chain[:, sites:, :sites], 1, 2).astype(jnp.int32)
        offsets = whole[..., : site_offsets.shape[1]]
        entry = whole[..., 8 : 8 + coupling_index.shape[1]]
        layer_id = jnp.arange(1, total + 1, dtype=jnp.int32)[:, None, None]
        site_id = jnp.arange(sites, dtype=jnp.int32)[None, :, None]
        slots = entry.shape[2]
        one = 1 - 2 * x
        shifts = jnp.where(
            jnp.arange(slots) == slots - 2, -one, jnp.where(jnp.arange(slots) == slots - 1, one, 0)
        ).astype(jnp.int32)
        moved = jnp.concatenate([jnp.zeros_like(offsets[..., :1]), offsets], axis=2)
        source = (layer_id + shifts) * sites + (site_id + moved) % sites
        consts = (source.reshape(-1), entry.reshape(-1), x_arr, table, pot)
        degree = lax.dynamic_slice_in_dim(degrees, x * half, half)
        degree = jnp.broadcast_to(degree[:, None], (half, orb))

    inside = list(range(2, total))

    def sent_after(value):
        mark = call(mark_body, (), [], jax.ShapeDtypeStruct((8, orb), f32), after=(value,))
        return swap(mark, "c")
    group = ("x",) + states_axes

    def regroup(value, axes):
        flat = value.reshape((-1,) + value.shape[2:])
        return lax.all_to_all(flat, axes, 0, 0, tiled=True).reshape(value.shape)

    own_order, their_order = list(range(2, layers + 1)), list(range(layers + 1, total))
    theirs = partner_i[::-1]
    with jax.named_scope("first"):
        four1 = step(
            consts, [partner_b, theirs, far], [[total], their_order, [total + 1]], [total], total,
            after=(ends,),
        )
        near1 = z_move(four1, False)
        one1 = step(consts, [mine_b, mine_i, near], [[1], own_order, [0]], [1], total, after=(four1,))
        far1 = z_move(one1, True)
        in1 = step(
            consts, [mine_b, mine_i, theirs, partner_b], [[1], own_order, their_order, [total]],
            inside, total, after=(one1,),
        )
    start_in = jnp.concatenate([mine_i, theirs], axis=0)
    with jax.named_scope("second"):
        one2, one1s = step(
            consts, [one1, in1, near1], [[1], inside, [0]], [1], total,
            [ends, mine_b, start_in, near], number=2,
        )
        far2 = z_move(one2, True)
        in2, in1s = step(
            consts, [one1, in1, four1], [[1], inside, [total]], inside, total,
            [ends, mine_b, start_in, partner_b], number=2, after=(sent_after(one2),),
        )
        four2, four1 = step(
            consts, [four1, in1, far1], [[total], inside, [total + 1]], [total], total,
            [ends, partner_b, start_in, far], number=2, after=(in2,),
        )
    in1 = in1s
    with jax.named_scope("third"):
        near2 = z_move(four2, False)
        in3_local = step(
            consts, [one2, in2, four2], [[1], inside, [total]], inside, total,
            [ends, in1, degree], (2, states, layers - 1, share, half, orb), number=3,
            after=(sent_after(four2),),
        )
        in3 = regroup(in3_local, group)
        edge_shape = (2, states, 1, share, half, orb)
        four3 = step(
            consts, [four2, in2, far2], [[total], inside, [total + 1]], [total], total,
            [ends, four1, degree], edge_shape, number=3, after=(in3_local,),
        )
        out3 = step(
            consts, [one2, in2, near2], [[1], inside, [0]], [1], total,
            [ends, one1s, degree], edge_shape, number=3, cost=large, into=four3,
        )
        out3 = regroup(out3, group)
    pieces = (out3, in3)
    width = 2 * states * half
    depth_rows = layers * share * orb
    tiles = width // orb
    with jax.named_scope("gram"):
        gram = call(
            gram_body,
            pieces,
            [vmem()] * 2,
            jax.ShapeDtypeStruct((tiles * (tiles + 1) // 2 * orb, orb), f32),
            [pltpu.VMEM((width, depth_rows), bf16)] * 2,
        )
        high, low = call(
            rows_body,
            (x_arr, *pieces),
            [smem()] + [vmem()] * 2,
            [jax.ShapeDtypeStruct((layers, share, orb, width), bf16)] * 2,
        )
        gram = group_sum(gram, [("c",), ("x", "y"), ("z",)])
    with jax.named_scope("finish"):
        return call(
            finish_body,
            (gram, high, low),
            [vmem()] * 3,
            jax.ShapeDtypeStruct((layers, share, orb, width), f32),
            [
                pltpu.VMEM((width, width), f32),
                pltpu.VMEM((orb, orb), f32),
                pltpu.VMEM((orb, orb), f32),
                pltpu.VMEM((orb, width), f32),
                pltpu.VMEM((width, 2 * width), bf16),
            ],
        )


def solution(mesh):
    blk, states = mesh.shape["blk"], mesh.shape["states"]
    grid = Mesh(
        np.asarray(mesh.devices).reshape(blk // 2, 2, states // 2, 2), ("z", "x", "y", "c")
    )
    b, s = ("z", "x"), ("y", "c")
    in_specs = (
        P(b, None, None, s),
        P(),
        P(b, None, None),
        P(b, None, None),
        P(b, None, None),
        P(s),
    )
    return jax.shard_map(
        per_device, mesh=grid, in_specs=in_specs, out_specs=P(b, s, None, None), check_vma=False
    )
```

```python
import functools

import jax
import jax.numpy as jnp
import numpy as np
from jax import lax
from jax.experimental import pallas as pl
from jax.experimental.pallas import tpu as pltpu
from jax.sharding import Mesh
from jax.sharding import PartitionSpec as P

cut_share = 0.3
exact = lax.Precision.HIGHEST
f32 = jnp.float32
bf16 = jnp.bfloat16
pivots = 4
strip = 64
vmem_limit = 12 * 1024 * 1024
small = pl.CostEstimate(flops=1, bytes_accessed=1, transcendentals=0)
large = pl.CostEstimate(flops=2 * 10**11, bytes_accessed=1, transcendentals=0)
NT = (((1,), (1,)), ((), ()))
TN = (((0,), (0,)), ((), ()))


def vmem():
    return pl.BlockSpec(memory_space=pltpu.VMEM)


def smem():
    return pl.BlockSpec(memory_space=pltpu.SMEM)


def call(body, args, specs, out_shape, scratch=(), after=(), cost=small):
    skipped = len(after)

    def kernel(*refs):
        body(*refs[: len(args)], *refs[len(args) + skipped :])

    return pl.pallas_call(
        kernel,
        out_shape=out_shape,
        in_specs=[*specs, *[pl.BlockSpec(memory_space=pl.ANY)] * skipped],
        out_specs=jax.tree.map(lambda _: vmem(), out_shape),
        scratch_shapes=list(scratch),
        compiler_params=pltpu.CompilerParams(vmem_limit_bytes=vmem_limit),
        cost_estimate=cost,
    )(*args, *after)


def halves(value):
    high = value.astype(bf16)
    return high, (value - high.astype(f32)).astype(bf16)


def hold(value, *after):
    def kernel(*refs):
        pass

    return pl.pallas_call(
        kernel,
        out_shape=jax.ShapeDtypeStruct(value.shape, value.dtype),
        in_specs=[pl.BlockSpec(memory_space=pl.ANY)] * (1 + len(after)),
        out_specs=pl.BlockSpec(memory_space=pl.ANY),
        input_output_aliases={0: 0},
        cost_estimate=small,
    )(value, *after)


def swap(value, axis):
    return lax.ppermute(value, axis, [(0, 1), (1, 0)])


def turn_body(first, x_ref, v_ref, *refs):
    mine, other = refs[-2:]
    layers, sites, _, count = v_ref.shape
    half = count // 2
    x = x_ref[0]
    for j in range(mine.shape[0]):
        layer = x * (layers - 1) + (1 - 2 * x) * (first + j) if layers > 1 else 0

        def one(s, carry):
            turned = v_ref[layer, s].T
            low, high = turned[:half], turned[half:]
            mine[j, s] = jnp.where(x == 0, low, high)
            other[j, s] = jnp.where(x == 0, high, low)
            return carry

        lax.fori_loop(0, sites, one, 0, unroll=4)


def turn_first(x_arr, states):
    layers, sites, orb, count = states.shape

    def kernel(x_ref, v_ref, mine, other, mark):
        turn_body(0, x_ref, v_ref, mine, other)
        mark[...] = jnp.zeros_like(mark)

    shape = (1, sites, count // 2, orb)
    return pl.pallas_call(
        kernel,
        out_shape=[jax.ShapeDtypeStruct(shape, f32)] * 2 + [jax.ShapeDtypeStruct((8, orb), f32)],
        grid_spec=pltpu.PrefetchScalarGridSpec(
            num_scalar_prefetch=1,
            grid=(1,),
            in_specs=[
                pl.BlockSpec((1, sites, orb, count), lambda i, x: (x[0] * (layers - 1), 0, 0, 0))
            ],
            out_specs=[pl.BlockSpec(shape, lambda i, x: (0, 0, 0, 0))] * 2
            + [pl.BlockSpec((8, orb), lambda i, x: (0, 0))],
        ),
        compiler_params=pltpu.CompilerParams(vmem_limit_bytes=vmem_limit),
        cost_estimate=small,
    )(x_arr, states)


def mark_body(out_ref):
    out_ref[...] = jnp.zeros_like(out_ref)


def lists_body(x_ref, pot_ref, offset_ref, entry_ref, out_ref):
    layers, sites, _ = pot_ref.shape
    x = x_ref[0]
    out_ref[...] = jnp.zeros_like(out_ref)
    for j in range(layers):
        layer = x * (layers - 1) + (1 - 2 * x) * j
        out_ref[j, :sites, :] = pot_ref[layer]
        row = sites
        for ref in (offset_ref, entry_ref):
            out_ref[j, row : row + ref.shape[1], :sites] = ref[layer].astype(f32)
            row += 8


def table_body(index_ref, coup_ref, pot_ref, table_ref, ends_ref, row_abs, diag):
    entries, orb, _ = coup_ref.shape
    rows = lax.broadcasted_iota(jnp.int32, (orb, orb), 0)
    cols = lax.broadcasted_iota(jnp.int32, (orb, orb), 1)

    def entry(c, carry):
        turned = coup_ref[c].T
        high, low = halves(turned)
        table_ref[c, :, :orb] = high
        table_ref[c, :, orb:] = low
        row_abs[c] = jnp.sum(jnp.abs(turned), axis=0, keepdims=True)
        diag[c] = jnp.sum(jnp.where(rows == cols, turned, 0.0), axis=0, keepdims=True)
        return carry

    lax.fori_loop(0, entries, entry, 0)
    layers, sites, _ = pot_ref.shape
    slots = index_ref.shape[0] // (layers * sites)

    def block(r, carry):
        top, low = carry
        layer, s = r // sites, lax.rem(r, sites)
        at = layer * slots * sites + s
        own = diag[index_ref[at]]
        center = own + pot_ref[layer, pl.ds(s, 1), :]
        radius = row_abs[index_ref[at]] - jnp.abs(own)
        for k in range(1, slots):
            radius = radius + row_abs[index_ref[at + k * sites]]
        return jnp.maximum(top, center + radius), jnp.maximum(low, radius - center)

    start = jnp.full((1, orb), -jnp.inf, f32)
    top, low = lax.fori_loop(0, layers * sites, block, (start, start))
    ends_ref[...] = jnp.concatenate(
        [jnp.broadcast_to(top, (4, orb)), jnp.broadcast_to(low, (4, orb))], axis=0
    )


def step_body(order, layers_out, total, number, last, *refs):
    refs = list(refs)
    take = lambda count: [refs.pop(0) for _ in range(count)]
    (source_ref, entry_ref, x_ref) = take(3)
    table_ref, pot_ref = take(2)
    pieces = take(len(order))
    ends_ref = take(1)[0] if number > 1 else None
    starts = take(len(order)) if number == 2 else []
    prev = take(1)[0] if number == 3 else None
    degree_ref = take(1)[0] if last else None
    split = refs.pop()
    scaled = refs.pop() if number == 2 else None
    out_ref = refs.pop() if not last else refs[-1]

    lookup, before_of = {}, {}
    for n, chain_layers in enumerate(order):
        for at, layer in enumerate(chain_layers):
            lookup[layer] = (pieces[n], at)
            before_of[layer] = (starts[n], at) if starts else None
    sites, half, orb = pieces[0].shape[1:]
    slots = source_ref.shape[0] // (total * sites)

    if number > 1:
        top = jnp.max(ends_ref[0:1, :], axis=1, keepdims=True)
        low = -jnp.max(ends_ref[4:5, :], axis=1, keepdims=True)
        cut_edge = low + cut_share * (top - low)
        middle = (top + cut_edge) / 2.0
        gain = 1.0 / ((top - cut_edge) / 2.0)

    def field_at(layer, s):
        piece, at = lookup[layer]
        if number != 2:
            return piece[at, s]
        start, at = before_of[layer]
        return (piece[at, s] - middle * start[at, s]) * gain

    for layer in lookup:

        def one(s, carry):
            high, low_part = halves(field_at(layer, s))
            split[layer * sites + s, :half, :] = high
            split[layer * sites + s, half:, :] = low_part
            return carry

        lax.fori_loop(0, sites, one, 0, unroll=4)

    for n, layer in enumerate(layers_out):

        def block(s, carry):
            row = (layer - 1) * sites + s
            left = [split[source_ref[row * slots + k]] for k in range(slots)]
            right = [table_ref[entry_ref[row * slots + k]] for k in range(slots)]
            both = jnp.dot(
                jnp.concatenate(left, axis=1),
                jnp.concatenate(right, axis=0),
                preferred_element_type=f32,
            )
            applied = both[:half, :orb] + (both[:half, orb:] + both[half:, :orb])
            field = field_at(layer, s)
            shift = pot_ref[pl.ds(row, 1), :]
            if number == 1:
                result = applied + shift * field
            else:
                start, start_at = before_of[layer] or (prev, n)
                before = start[start_at, s]
                result = (applied + (shift - middle) * field) * (2.0 * gain) - before
            if number == 2:
                scaled[n, s] = field
            if last:
                degree = degree_ref[...]
                result = jnp.where(degree == 1, before, jnp.where(degree == 2, field, result))
                share = out_ref.shape[3]
                own = layer <= total // 2
                place = max((layer - 1 if own else total - layer) - 1, 0)
                side = (x_ref[0] if own else 1 - x_ref[0]) if out_ref.shape[0] == 2 else 0
                out_ref[side, s // share, place, lax.rem(s, share)] = result
            else:
                out_ref[n, s] = result
            return carry

        lax.fori_loop(0, sites, block, 0, unroll=4)


def step(consts, pieces, order, layers_out, total, more=(), last_shape=None, number=1, after=(), cost=small, into=None):
    sites, half, orb = pieces[0].shape[1:]
    last = last_shape is not None
    shape = last_shape if last else (len(layers_out), sites, half, orb)
    args = [*consts, *pieces, *more]
    scratch = [pltpu.VMEM(((total + 2) * sites, 2 * half, orb), bf16)]
    body = functools.partial(step_body, order, layers_out, total, number, last)
    out = jax.ShapeDtypeStruct(shape, f32)
    one_side = last and len(layers_out) == 1
    if not one_side:
        specs = [smem()] * 3 + [vmem()] * (len(args) - 3)
        return call(body, args, specs, [out, out] if number == 2 else out, scratch, after, cost)
    own = layers_out[0] == 1
    extra = [*after] + ([into] if into is not None else [])
    count = len(args)

    def kernel(*refs):
        body(*refs[:count], *refs[count + len(extra) :])

    zeros = (0,) * (len(shape) - 1)
    return pl.pallas_call(
        kernel,
        out_shape=out,
        grid_spec=pltpu.PrefetchScalarGridSpec(
            num_scalar_prefetch=3,
            grid=(1,),
            in_specs=[vmem()] * (count - 3) + [pl.BlockSpec(memory_space=pl.ANY)] * len(extra),
            out_specs=pl.BlockSpec(
                (1, *shape[1:]), lambda i, a, b, x: (x[0] if own else 1 - x[0], *zeros)
            ),
            scratch_shapes=scratch,
        ),
        input_output_aliases={count + len(after): 0} if into is not None else {},
        compiler_params=pltpu.CompilerParams(vmem_limit_bytes=vmem_limit),
        cost_estimate=cost,
    )(*args, *extra)


def all_states(edge_ref, inner_ref, chain, s):
    ref, layer = (edge_ref, 0) if chain == 0 else (inner_ref, chain - 1)
    return [ref[a, b, layer, s] for b in range(ref.shape[1]) for a in range(2)]


def gram_body(edge_ref, inner_ref, gram_ref, high, low):
    _, _, inner_layers, share, half, orb = inner_ref.shape
    col = 0
    for chain in range(inner_layers + 1):
        for s in range(share):
            for n, part in enumerate(all_states(edge_ref, inner_ref, chain, s)):
                at = (slice(n * half, (n + 1) * half), slice(col, col + orb))
                high[at], low[at] = halves(part)
            col += orb
    count = high.shape[0]
    tile = gram_ref.shape[1]
    wide = 2 * tile
    place = 0
    blocks = {}
    for i in range(0, count, wide):
        for j in range(0, i + 1, wide):
            a = [r[i : i + wide, :] for r in (high, high, low)]
            b = [r[j : j + wide, :] for r in (high, low, high)]
            blocks[i, j] = lax.dot_general(
                jnp.concatenate(a, axis=1),
                jnp.concatenate(b, axis=1),
                NT,
                preferred_element_type=f32,
            )
    for i in range(0, count, tile):
        for j in range(0, i + 1, tile):
            block = blocks[i // wide * wide, j // wide * wide]
            gram_ref[place : place + tile, :] = block[
                i % wide : i % wide + tile, j % wide : j % wide + tile
            ]
            place += tile


def rows_body(x_ref, edge_ref, inner_ref, high, low):
    x = x_ref[0]
    layers, share = high.shape[:2]
    for chain in range(layers):
        natural = x * (layers - 1) + (1 - 2 * x) * chain
        for s in range(share):
            parts = all_states(edge_ref, inner_ref, chain, s)
            a, b = halves(jnp.concatenate(parts, axis=0).T)
            high[natural, s] = a
            low[natural, s] = b


def adjugate_4(a):
    def minor(i, j, m, n):
        return a[i][m] * a[j][n] - a[j][m] * a[i][n]

    pairs = [(0, 1), (0, 2), (0, 3), (1, 2), (1, 3), (2, 3)]
    s = [minor(0, 1, m, n) for m, n in pairs]
    c = [minor(2, 3, m, n) for m, n in pairs]
    det = (s[0] * c[5] - s[1] * c[4]) + (s[2] * c[3] + s[3] * c[2]) - (s[4] * c[1] - s[5] * c[0])
    b = [[None] * 4 for _ in range(4)]
    b[0][0] = a[1][1] * c[5] - a[1][2] * c[4] + a[1][3] * c[3]
    b[0][1] = a[0][2] * c[4] - a[0][1] * c[5] - a[0][3] * c[3]
    b[0][2] = a[3][1] * s[5] - a[3][2] * s[4] + a[3][3] * s[3]
    b[0][3] = a[2][2] * s[4] - a[2][1] * s[5] - a[2][3] * s[3]
    b[1][1] = a[0][0] * c[5] - a[0][2] * c[2] + a[0][3] * c[1]
    b[1][2] = a[3][2] * s[2] - a[3][0] * s[5] - a[3][3] * s[1]
    b[1][3] = a[2][0] * s[5] - a[2][2] * s[2] + a[2][3] * s[1]
    b[2][2] = a[3][0] * s[4] - a[3][1] * s[2] + a[3][3] * s[0]
    b[2][3] = a[2][1] * s[2] - a[2][0] * s[4] - a[2][3] * s[0]
    b[3][3] = a[2][0] * s[3] - a[2][1] * s[1] + a[2][2] * s[0]
    for i in range(4):
        for j in range(i):
            b[i][j] = b[j][i]
    return b, det


def lower_inverse_small(a):
    size = len(a)
    low = [[None] * size for _ in range(size)]
    scale = [None] * size
    for j in range(size):
        d = a[j][j]
        for k in range(j):
            d = d - low[j][k] * low[j][k]
        scale[j] = lax.rsqrt(d)
        for i in range(j + 1, size):
            v = a[i][j]
            for k in range(j):
                v = v - low[i][k] * low[j][k]
            low[i][j] = v * scale[j]
    inv = [[None] * size for _ in range(size)]
    for i in range(size):
        inv[i][i] = scale[i]
        for j in range(i):
            v = low[i][j] * inv[j][j]
            for k in range(j + 1, i):
                v = v + low[i][k] * inv[k][j]
            inv[i][j] = -(v * scale[i])
    return inv


def spread_lane(value, lane):
    return jnp.take_along_axis(
        value, jnp.full(value.shape, lane, jnp.int32), axis=1, mode="promise_in_bounds"
    )


def spread_row(value, row):
    return jnp.broadcast_to(value[row : row + 1, :], value.shape)


def lower_inverse(block_ref, out_ref):
    size = block_ref.shape[0]
    shape = (8, size)
    lanes = lax.broadcasted_iota(jnp.int32, shape, 1)
    subs = lax.broadcasted_iota(jnp.int32, shape, 0)
    rows = [block_ref[8 * g : 8 * g + 8, :] for g in range(size // 8)]
    for first in range(0, size, strip):
        past = (first + strip) // 8
        for start in range(first, first + strip, pivots):
            group, offset = divmod(start, 8)
            inside = (lanes >= start) & (lanes < start + pivots)
            here = rows[group]
            columns = {
                g: [spread_lane(rows[g], start + k) for k in range(pivots)]
                for g in range(group, past)
            }
            if start == first:
                corner = [
                    [spread_row(columns[group][j], offset + i) for j in range(pivots)]
                    for i in range(pivots)
                ]
            lines = [
                jnp.where(
                    inside,
                    jnp.where(lanes == start + k, 1.0, 0.0),
                    spread_row(here, offset + k),
                )
                for k in range(pivots)
            ]
            adj, det = adjugate_4(corner)
            share = 1.0 / det
            weights = [
                ((adj[k][0] * lines[0] + adj[k][1] * lines[1]) + (adj[k][2] * lines[2] + adj[k][3] * lines[3]))
                * share
                for k in range(pivots)
            ]
            after = start + pivots
            next_corner = None
            if after < first + strip:
                ng, noff = divmod(after, 8)
                side = [
                    [spread_row(columns[ng][k], noff + i) for k in range(pivots)]
                    for i in range(pivots)
                ]
                ahead = [spread_lane(rows[ng], after + j) for j in range(pivots)]
                part = [
                    [
                        (adj[k][0] * side[j][0] + adj[k][1] * side[j][1])
                        + (adj[k][2] * side[j][2] + adj[k][3] * side[j][3])
                        for j in range(pivots)
                    ]
                    for k in range(pivots)
                ]
                next_corner = [[None] * pivots for _ in range(pivots)]
                for i in range(pivots):
                    for j in range(i + 1):
                        taken = (side[i][0] * part[0][j] + side[i][1] * part[1][j]) + (
                            side[i][2] * part[2][j] + side[i][3] * part[3][j]
                        )
                        next_corner[i][j] = spread_row(ahead[j], noff + i) - taken * share
                        next_corner[j][i] = next_corner[i][j]
            for g in range(group, past):
                c = columns[g]
                change = (c[0] * weights[0] + c[1] * weights[1]) + (c[2] * weights[2] + c[3] * weights[3])
                updated = jnp.where(inside, 0.0, rows[g]) - change
                if g == group:
                    updated = jnp.where(subs >= offset + pivots, updated, rows[g])
                rows[g] = updated
            low = lower_inverse_small(corner)
            for r in range(pivots):
                line = functools.reduce(jnp.add, [low[r][k] * lines[k] for k in range(r + 1)])
                rows[group] = jnp.where(subs == offset + r, line, rows[group])
            corner = next_corner
        mine = (lanes >= first) & (lanes < first + strip)
        for g in range(first // 8, past):
            rows[g] = jnp.where(mine & (lanes > subs + 8 * g), 0.0, rows[g])
            out_ref[8 * g : 8 * g + 8, :] = jnp.where(lanes <= subs + 8 * g, rows[g], 0.0)
        if past < size // 8:
            panel = jnp.concatenate(rows[first // 8 : past], axis=0)
            high, low_part = halves(panel)
            wide = jnp.concatenate([high, low_part, high], axis=0)
            tall = jnp.concatenate([high, high, low_part], axis=0).astype(f32)
            tall = jnp.concatenate([tall, jnp.zeros((-3 * strip % size, size), f32)], axis=0).T
            change = jnp.dot(
                tall[first + strip :, : 3 * strip].astype(bf16), wide, preferred_element_type=f32
            )
            for n, g in enumerate(range(past, size // 8)):
                rows[g] = jnp.where(mine, 0.0, rows[g]) - change[8 * n : 8 * n + 8, :]


def three(left, right):
    a, b = halves(left)
    c, d = halves(right)
    return jnp.dot(
        jnp.concatenate([a, a, b], axis=1),
        jnp.concatenate([c, d, c], axis=0),
        preferred_element_type=f32,
    )


def finish_body(gram_ref, high_ref, low_ref, out_ref, work, diag, lower, panel, inv):
    size = work.shape[0]
    tile = diag.shape[0]
    eye = lax.broadcasted_iota(jnp.int32, (tile, tile), 0) == lax.broadcasted_iota(
        jnp.int32, (tile, tile), 1
    )
    down, across = [], []
    place = -tile
    for i in range(0, size, tile):
        place += i + tile
        kept = jnp.where(eye, gram_ref[place : place + tile, :], 0.0)
        down.append(lax.rsqrt(jnp.sum(kept, axis=1, keepdims=True)))
        across.append(lax.rsqrt(jnp.sum(kept, axis=0, keepdims=True)))
    scales = jnp.concatenate(across, axis=1)
    place = 0
    for i in range(0, size, tile):
        for j in range(0, i + 1, tile):
            block = gram_ref[place : place + tile, :] * down[i // tile] * across[j // tile]
            place += tile
            work[i : i + tile, j : j + tile] = block
            if i != j:
                work[j : j + tile, i : i + tile] = block.T
    cols = lax.broadcasted_iota(jnp.int32, (tile, size), 1)
    local = lax.broadcasted_iota(jnp.int32, (tile, size), 0)

    def outer(b, carry):
        at = pl.multiple_of(b * tile, tile)
        diag[...] = work[pl.ds(at, tile), pl.ds(at, tile)]
        lower_inverse(diag, lower)
        inside = (cols >= at) & (cols < at + tile)
        line = jnp.where(
            inside, jnp.where(cols - at == local, 1.0, 0.0), work[pl.ds(at, tile), :]
        )
        panel[...] = three(lower[...], line)
        kept = jnp.where(cols < at + tile, panel[...] * scales, 0.0)
        high, low = halves(kept)
        inv[pl.ds(at, tile), :size] = high
        inv[pl.ds(at, tile), size:] = low

        def trailing(i, carry):
            to = pl.multiple_of(i * tile, tile)
            change = three(panel[:, pl.ds(to, tile)].T, panel[...])
            work[pl.ds(to, tile), :] = jnp.where(inside, 0.0, work[pl.ds(to, tile), :]) - change
            return carry

        lax.fori_loop(b + 1, size // tile, trailing, 0)
        return carry

    lax.fori_loop(0, size // tile, outer, 0)

    layers, share, orb, _ = out_ref.shape

    def result(s, carry):
        a = jnp.concatenate([high_ref[n, s] for n in range(layers)], axis=0)
        b = jnp.concatenate([low_ref[n, s] for n in range(layers)], axis=0)
        for first in range(0, size, 2 * tile):
            last = first + 2 * tile
            c = inv[first:last, :last]
            d = inv[first:last, size : size + last]
            total = lax.dot_general(
                jnp.concatenate([a[:, :last], a[:, :last], b[:, :last]], axis=1),
                jnp.concatenate([c, d, c], axis=1),
                NT,
                preferred_element_type=f32,
            )
            for n in range(layers):
                out_ref[n, s, :, first:last] = total[n * orb : (n + 1) * orb]
        return carry

    lax.fori_loop(0, share, result, 0)


def group_sum(value, axis_sets):
    if not axis_sets:
        return value
    axes, *rest = axis_sets
    count = lax.axis_size(axes)
    if count == 1:
        return group_sum(value, rest)
    if not rest and count & (count - 1) == 0:
        hop = 1
        while hop < count:
            value = value + lax.ppermute(value, axes, [(i, i ^ hop) for i in range(count)])
            hop *= 2
        return value
    if count > 8 or value.shape[0] % (8 * count):
        return group_sum(lax.psum(value, axes), rest)
    me = lax.axis_index(axes)
    share = value.shape[0] // count

    def piece(k):
        return lax.dynamic_slice_in_dim(value, lax.rem(me + k, count) * share, share, axis=0)

    total = piece(0)
    got = [
        lax.ppermute(piece(k), axes, [(i, (i + k) % count) for i in range(count)])
        for k in range(1, count)
    ]
    for part in got:
        total = total + part
    total = group_sum(total, rest)
    back = [
        lax.ppermute(total, axes, [(i, (i - k) % count) for i in range(count)])
        for k in range(1, count)
    ]
    out = jnp.zeros_like(value)
    out = lax.dynamic_update_slice_in_dim(out, total, me * share, axis=0)
    for k, part in enumerate(back, 1):
        out = lax.dynamic_update_slice_in_dim(out, part, lax.rem(me + k, count) * share, axis=0)
    return out


def per_device(start_states, couplings, potential, site_offsets, coupling_index, degrees):
    layers, sites, orb, count = start_states.shape
    half = count // 2
    total = 2 * layers
    x = lax.axis_index("x").astype(jnp.int32)
    x_arr = x[None]
    depth = lax.axis_size("z")
    states_axes = ("y", "c")
    states = lax.axis_size(states_axes)
    share = sites // states

    def z_move(value, near):
        pairs = []
        for z in range(depth):
            for xx in range(2):
                d = (1 if xx else -1) * (1 if near else -1)
                pairs.append((z * 2 + xx, (z + d) % depth * 2 + xx))
        return lax.ppermute(value, ("z", "x"), pairs)

    with jax.named_scope("prepare"):
        mine_b, other_b, mark = turn_first(x_arr, start_states)
        far = z_move(mine_b, True)
        partner_b = swap(other_b, "x")
        mark = swap(mark, "c")
        lists = call(
            lists_body,
            (x_arr, potential, site_offsets, coupling_index),
            [smem(), vmem(), vmem(), vmem()],
            jax.ShapeDtypeStruct((layers, sites + 16, orb), f32),
            after=(mine_b,),
        )
        their_lists = swap(lists, "x")
        mine_i, other_i = call(
            functools.partial(turn_body, 1),
            (x_arr, start_states),
            [smem(), vmem()],
            [jax.ShapeDtypeStruct((layers - 1, sites, half, orb), f32)] * 2,
            after=(mine_b,),
        )
        table, ends = call(
            table_body,
            (coupling_index.reshape(-1), couplings, potential),
            [smem(), vmem(), vmem()],
            [
                jax.ShapeDtypeStruct((couplings.shape[0], orb, 2 * orb), bf16),
                jax.ShapeDtypeStruct((8, orb), f32),
            ],
            [pltpu.VMEM((couplings.shape[0], 1, orb), f32)] * 2,
            after=(mark,),
        )
        partner_b = hold(partner_b, far, table)
        devices = 2 * depth
        ends = jnp.broadcast_to(ends[None], (devices, *ends.shape))
        ends = jnp.max(lax.all_to_all(ends, ("z", "x"), 0, 0, tiled=True), axis=0)
        near = z_move(partner_b, False)
        partner_i = swap(hold(other_i, partner_b), "x")
        chain = jnp.concatenate([lists, their_lists[::-1]], axis=0)
        pot = chain[:, :sites].reshape(total * sites, orb)
        whole = jnp.swapaxes(chain[:, sites:, :sites], 1, 2).astype(jnp.int32)
        offsets = whole[..., : site_offsets.shape[1]]
        entry = whole[..., 8 : 8 + coupling_index.shape[1]]
        layer_id = jnp.arange(1, total + 1, dtype=jnp.int32)[:, None, None]
        site_id = jnp.arange(sites, dtype=jnp.int32)[None, :, None]
        slots = entry.shape[2]
        one = 1 - 2 * x
        shifts = jnp.where(
            jnp.arange(slots) == slots - 2, -one, jnp.where(jnp.arange(slots) == slots - 1, one, 0)
        ).astype(jnp.int32)
        moved = jnp.concatenate([jnp.zeros_like(offsets[..., :1]), offsets], axis=2)
        source = (layer_id + shifts) * sites + (site_id + moved) % sites
        consts = (source.reshape(-1), entry.reshape(-1), x_arr, table, pot)
        degree = lax.dynamic_slice_in_dim(degrees, x * half, half)
        degree = jnp.broadcast_to(degree[:, None], (half, orb))

    inside = list(range(2, total))

    def sent_after(value):
        mark = call(mark_body, (), [], jax.ShapeDtypeStruct((8, orb), f32), after=(value,))
        return swap(mark, "c")
    group = ("x",) + states_axes

    def regroup(value, axes):
        flat = value.reshape((-1,) + value.shape[2:])
        return lax.all_to_all(flat, axes, 0, 0, tiled=True).reshape(value.shape)

    own_order, their_order = list(range(2, layers + 1)), list(range(layers + 1, total))
    theirs = partner_i[::-1]
    with jax.named_scope("first"):
        four1 = step(
            consts, [partner_b, theirs, far], [[total], their_order, [total + 1]], [total], total,
            after=(ends,),
        )
        near1 = z_move(four1, False)
        one1 = step(consts, [mine_b, mine_i, near], [[1], own_order, [0]], [1], total, after=(four1,))
        far1 = z_move(one1, True)
        in1 = step(
            consts, [mine_b, mine_i, theirs, partner_b], [[1], own_order, their_order, [total]],
            inside, total, after=(one1,),
        )
    start_in = jnp.concatenate([mine_i, theirs], axis=0)
    with jax.named_scope("second"):
        one2, one1s = step(
            consts, [one1, in1, near1], [[1], inside, [0]], [1], total,
            [ends, mine_b, start_in, near], number=2,
        )
        far2 = z_move(one2, True)
        in2, in1s = step(
            consts, [one1, in1, four1], [[1], inside, [total]], inside, total,
            [ends, mine_b, start_in, partner_b], number=2, after=(sent_after(one2),),
        )
        four2, four1 = step(
            consts, [four1, in1, far1], [[total], inside, [total + 1]], [total], total,
            [ends, partner_b, start_in, far], number=2, after=(in2,),
        )
    in1 = in1s
    with jax.named_scope("third"):
        near2 = z_move(four2, False)
        in3_local = step(
            consts, [one2, in2, four2], [[1], inside, [total]], inside, total,
            [ends, in1, degree], (2, states, layers - 1, share, half, orb), number=3,
            after=(sent_after(four2),),
        )
        in3 = regroup(in3_local, group)
        edge_shape = (2, states, 1, share, half, orb)
        four3 = step(
            consts, [four2, in2, far2], [[total], inside, [total + 1]], [total], total,
            [ends, four1, degree], edge_shape, number=3, after=(in3_local,),
        )
        out3 = step(
            consts, [one2, in2, near2], [[1], inside, [0]], [1], total,
            [ends, one1s, degree], edge_shape, number=3, cost=large, into=four3,
        )
        out3 = regroup(out3, group)
    pieces = (out3, in3)
    width = 2 * states * half
    depth_rows = layers * share * orb
    tiles = width // orb
    with jax.named_scope("gram"):
        gram = call(
            gram_body,
            pieces,
            [vmem()] * 2,
            jax.ShapeDtypeStruct((tiles * (tiles + 1) // 2 * orb, orb), f32),
            [pltpu.VMEM((width, depth_rows), bf16)] * 2,
        )
        high, low = call(
            rows_body,
            (x_arr, *pieces),
            [smem()] + [vmem()] * 2,
            [jax.ShapeDtypeStruct((layers, share, orb, width), bf16)] * 2,
        )
        gram = group_sum(gram, [("c",), ("x", "y"), ("z",)])
    with jax.named_scope("finish"):
        return call(
            finish_body,
            (gram, high, low),
            [vmem()] * 3,
            jax.ShapeDtypeStruct((layers, share, orb, width), f32),
            [
                pltpu.VMEM((width, width), f32),
                pltpu.VMEM((orb, orb), f32),
                pltpu.VMEM((orb, orb), f32),
                pltpu.VMEM((orb, width), f32),
                pltpu.VMEM((width, 2 * width), bf16),
            ],
        )


def solution(mesh):
    blk, states = mesh.shape["blk"], mesh.shape["states"]
    grid = Mesh(
        np.asarray(mesh.devices).reshape(blk // 2, 2, states // 2, 2), ("z", "x", "y", "c")
    )
    b, s = ("z", "x"), ("y", "c")
    in_specs = (
        P(b, None, None, s),
        P(),
        P(b, None, None),
        P(b, None, None),
        P(b, None, None),
        P(s),
    )
    return jax.shard_map(
        per_device, mesh=grid, in_specs=in_specs, out_specs=P(b, s, None, None), check_vma=False
    )
```

```python
import functools

import jax
import jax.numpy as jnp
import numpy as np
from jax import lax
from jax.experimental import pallas as pl
from jax.experimental.pallas import tpu as pltpu
from jax.sharding import Mesh
from jax.sharding import PartitionSpec as P

cut_share = 0.3
exact = lax.Precision.HIGHEST
f32 = jnp.float32
bf16 = jnp.bfloat16
pivots = 4
strip = 64
vmem_limit = 12 * 1024 * 1024
small = pl.CostEstimate(flops=1, bytes_accessed=1, transcendentals=0)
large = pl.CostEstimate(flops=2 * 10**11, bytes_accessed=1, transcendentals=0)
NT = (((1,), (1,)), ((), ()))
TN = (((0,), (0,)), ((), ()))


def vmem():
    return pl.BlockSpec(memory_space=pltpu.VMEM)


def smem():
    return pl.BlockSpec(memory_space=pltpu.SMEM)


def call(body, args, specs, out_shape, scratch=(), after=(), cost=small):
    skipped = len(after)

    def kernel(*refs):
        body(*refs[: len(args)], *refs[len(args) + skipped :])

    return pl.pallas_call(
        kernel,
        out_shape=out_shape,
        in_specs=[*specs, *[pl.BlockSpec(memory_space=pl.ANY)] * skipped],
        out_specs=jax.tree.map(lambda _: vmem(), out_shape),
        scratch_shapes=list(scratch),
        compiler_params=pltpu.CompilerParams(vmem_limit_bytes=vmem_limit),
        cost_estimate=cost,
    )(*args, *after)


def halves(value):
    high = value.astype(bf16)
    return high, (value - high.astype(f32)).astype(bf16)


def hold(value, *after):
    def kernel(*refs):
        pass

    return pl.pallas_call(
        kernel,
        out_shape=jax.ShapeDtypeStruct(value.shape, value.dtype),
        in_specs=[pl.BlockSpec(memory_space=pl.ANY)] * (1 + len(after)),
        out_specs=pl.BlockSpec(memory_space=pl.ANY),
        input_output_aliases={0: 0},
        cost_estimate=small,
    )(value, *after)


def swap(value, axis):
    return lax.ppermute(value, axis, [(0, 1), (1, 0)])


def turn_body(first, x_ref, v_ref, *refs):
    mine, other = refs[-2:]
    layers, sites, _, count = v_ref.shape
    half = count // 2
    x = x_ref[0]
    for j in range(mine.shape[0]):
        layer = x * (layers - 1) + (1 - 2 * x) * (first + j) if layers > 1 else 0

        def one(s, carry):
            turned = v_ref[layer, s].T
            low, high = turned[:half], turned[half:]
            mine[j, s] = jnp.where(x == 0, low, high)
            other[j, s] = jnp.where(x == 0, high, low)
            return carry

        lax.fori_loop(0, sites, one, 0, unroll=4)


def turn_first(x_arr, states):
    layers, sites, orb, count = states.shape

    def kernel(x_ref, v_ref, mine, other, mark):
        turn_body(0, x_ref, v_ref, mine, other)
        mark[...] = jnp.zeros_like(mark)

    shape = (1, sites, count // 2, orb)
    return pl.pallas_call(
        kernel,
        out_shape=[jax.ShapeDtypeStruct(shape, f32)] * 2 + [jax.ShapeDtypeStruct((8, orb), f32)],
        grid_spec=pltpu.PrefetchScalarGridSpec(
            num_scalar_prefetch=1,
            grid=(1,),
            in_specs=[
                pl.BlockSpec((1, sites, orb, count), lambda i, x: (x[0] * (layers - 1), 0, 0, 0))
            ],
            out_specs=[pl.BlockSpec(shape, lambda i, x: (0, 0, 0, 0))] * 2
            + [pl.BlockSpec((8, orb), lambda i, x: (0, 0))],
        ),
        compiler_params=pltpu.CompilerParams(vmem_limit_bytes=vmem_limit),
        cost_estimate=small,
    )(x_arr, states)


def mark_body(out_ref):
    out_ref[...] = jnp.zeros_like(out_ref)


def lists_body(x_ref, pot_ref, offset_ref, entry_ref, out_ref):
    layers, sites, _ = pot_ref.shape
    x = x_ref[0]
    out_ref[...] = jnp.zeros_like(out_ref)
    for j in range(layers):
        layer = x * (layers - 1) + (1 - 2 * x) * j
        out_ref[j, :sites, :] = pot_ref[layer]
        row = sites
        for ref in (offset_ref, entry_ref):
            out_ref[j, row : row + ref.shape[1], :sites] = ref[layer].astype(f32)
            row += 8


def table_body(index_ref, coup_ref, pot_ref, table_ref, ends_ref, row_abs, diag):
    entries, orb, _ = coup_ref.shape
    rows = lax.broadcasted_iota(jnp.int32, (orb, orb), 0)
    cols = lax.broadcasted_iota(jnp.int32, (orb, orb), 1)

    def entry(c, carry):
        turned = coup_ref[c].T
        high, low = halves(turned)
        table_ref[c, :, :orb] = high
        table_ref[c, :, orb:] = low
        row_abs[c] = jnp.sum(jnp.abs(turned), axis=0, keepdims=True)
        diag[c] = jnp.sum(jnp.where(rows == cols, turned, 0.0), axis=0, keepdims=True)
        return carry

    lax.fori_loop(0, entries, entry, 0)
    layers, sites, _ = pot_ref.shape
    slots = index_ref.shape[0] // (layers * sites)

    def block(r, carry):
        top, low = carry
        layer, s = r // sites, lax.rem(r, sites)
        at = layer * slots * sites + s
        own = diag[index_ref[at]]
        center = own + pot_ref[layer, pl.ds(s, 1), :]
        radius = row_abs[index_ref[at]] - jnp.abs(own)
        for k in range(1, slots):
            radius = radius + row_abs[index_ref[at + k * sites]]
        return jnp.maximum(top, center + radius), jnp.maximum(low, radius - center)

    start = jnp.full((1, orb), -jnp.inf, f32)
    top, low = lax.fori_loop(0, layers * sites, block, (start, start))
    ends_ref[...] = jnp.concatenate(
        [jnp.broadcast_to(top, (4, orb)), jnp.broadcast_to(low, (4, orb))], axis=0
    )


def step_body(order, layers_out, total, number, last, *refs):
    refs = list(refs)
    take = lambda count: [refs.pop(0) for _ in range(count)]
    (source_ref, entry_ref, x_ref) = take(3)
    table_ref, pot_ref = take(2)
    pieces = take(len(order))
    ends_ref = take(1)[0] if number > 1 else None
    starts = take(len(order)) if number == 2 else []
    prev = take(1)[0] if number == 3 else None
    degree_ref = take(1)[0] if last else None
    split = refs.pop()
    scaled = refs.pop() if number == 2 else None
    out_ref = refs.pop() if not last else refs[-1]

    lookup, before_of = {}, {}
    for n, chain_layers in enumerate(order):
        for at, layer in enumerate(chain_layers):
            lookup[layer] = (pieces[n], at)
            before_of[layer] = (starts[n], at) if starts else None
    sites, half, orb = pieces[0].shape[1:]
    slots = source_ref.shape[0] // (total * sites)

    if number > 1:
        top = jnp.max(ends_ref[0:1, :], axis=1, keepdims=True)
        low = -jnp.max(ends_ref[4:5, :], axis=1, keepdims=True)
        cut_edge = low + cut_share * (top - low)
        middle = (top + cut_edge) / 2.0
        gain = 1.0 / ((top - cut_edge) / 2.0)

    def field_at(layer, s):
        piece, at = lookup[layer]
        if number != 2:
            return piece[at, s]
        start, at = before_of[layer]
        return (piece[at, s] - middle * start[at, s]) * gain

    for layer in lookup:

        def one(s, carry):
            high, low_part = halves(field_at(layer, s))
            split[layer * sites + s, :half, :] = high
            split[layer * sites + s, half:, :] = low_part
            return carry

        lax.fori_loop(0, sites, one, 0, unroll=4)

    for n, layer in enumerate(layers_out):

        def block(s, carry):
            row = (layer - 1) * sites + s
            left = [split[source_ref[row * slots + k]] for k in range(slots)]
            right = [table_ref[entry_ref[row * slots + k]] for k in range(slots)]
            both = jnp.dot(
                jnp.concatenate(left, axis=1),
                jnp.concatenate(right, axis=0),
                preferred_element_type=f32,
            )
            applied = both[:half, :orb] + (both[:half, orb:] + both[half:, :orb])
            field = field_at(layer, s)
            shift = pot_ref[pl.ds(row, 1), :]
            if number == 1:
                result = applied + shift * field
            else:
                start, start_at = before_of[layer] or (prev, n)
                before = start[start_at, s]
                result = (applied + (shift - middle) * field) * (2.0 * gain) - before
            if number == 2:
                scaled[n, s] = field
            if last:
                degree = degree_ref[...]
                result = jnp.where(degree == 1, before, jnp.where(degree == 2, field, result))
                share = out_ref.shape[3]
                own = layer <= total // 2
                place = max((layer - 1 if own else total - layer) - 1, 0)
                side = (x_ref[0] if own else 1 - x_ref[0]) if out_ref.shape[0] == 2 else 0
                out_ref[side, s // share, place, lax.rem(s, share)] = result
            else:
                out_ref[n, s] = result
            return carry

        lax.fori_loop(0, sites, block, 0, unroll=16)


def step(consts, pieces, order, layers_out, total, more=(), last_shape=None, number=1, after=(), cost=small, into=None):
    sites, half, orb = pieces[0].shape[1:]
    last = last_shape is not None
    shape = last_shape if last else (len(layers_out), sites, half, orb)
    args = [*consts, *pieces, *more]
    scratch = [pltpu.VMEM(((total + 2) * sites, 2 * half, orb), bf16)]
    body = functools.partial(step_body, order, layers_out, total, number, last)
    out = jax.ShapeDtypeStruct(shape, f32)
    one_side = last and len(layers_out) == 1
    if not one_side:
        specs = [smem()] * 3 + [vmem()] * (len(args) - 3)
        return call(body, args, specs, [out, out] if number == 2 else out, scratch, after, cost)
    own = layers_out[0] == 1
    extra = [*after] + ([into] if into is not None else [])
    count = len(args)

    def kernel(*refs):
        body(*refs[:count], *refs[count + len(extra) :])

    zeros = (0,) * (len(shape) - 1)
    return pl.pallas_call(
        kernel,
        out_shape=out,
        grid_spec=pltpu.PrefetchScalarGridSpec(
            num_scalar_prefetch=3,
            grid=(1,),
            in_specs=[vmem()] * (count - 3) + [pl.BlockSpec(memory_space=pl.ANY)] * len(extra),
            out_specs=pl.BlockSpec(
                (1, *shape[1:]), lambda i, a, b, x: (x[0] if own else 1 - x[0], *zeros)
            ),
            scratch_shapes=scratch,
        ),
        input_output_aliases={count + len(after): 0} if into is not None else {},
        compiler_params=pltpu.CompilerParams(vmem_limit_bytes=vmem_limit),
        cost_estimate=cost,
    )(*args, *extra)


def all_states(edge_ref, inner_ref, chain, s):
    ref, layer = (edge_ref, 0) if chain == 0 else (inner_ref, chain - 1)
    return [ref[a, b, layer, s] for b in range(ref.shape[1]) for a in range(2)]


def gram_body(piece_ref, *refs):
    *given, gram_ref, high, low = refs
    _, states, layers, share, half, orb = piece_ref.shape
    col = 0
    for layer in range(layers):
        for s in range(share):
            for n in range(2 * states):
                at = (slice(n * half, (n + 1) * half), slice(col, col + orb))
                high[at], low[at] = halves(piece_ref[n % 2, n // 2, layer, s])
            col += orb
    count = high.shape[0]
    tile = gram_ref.shape[1]
    wide = 2 * tile
    place = 0
    blocks = {}
    for i in range(0, count, wide):
        for j in range(0, i + 1, wide):
            a = [r[i : i + wide, :] for r in (high, high, low, low)]
            b = [r[j : j + wide, :] for r in (high, low, high, low)]
            blocks[i, j] = lax.dot_general(
                jnp.concatenate(a, axis=1),
                jnp.concatenate(b, axis=1),
                NT,
                preferred_element_type=f32,
            )
    for i in range(0, count, tile):
        for j in range(0, i + 1, tile):
            block = blocks[i // wide * wide, j // wide * wide]
            block = block[i % wide : i % wide + tile, j % wide : j % wide + tile]
            for ref in given:
                block = block + ref[place : place + tile, :]
            gram_ref[place : place + tile, :] = block
            place += tile


def rows_body(x_ref, edge_ref, inner_ref, high, low):
    x = x_ref[0]
    layers, share = high.shape[:2]
    for chain in range(layers):
        natural = x * (layers - 1) + (1 - 2 * x) * chain
        for s in range(share):
            parts = all_states(edge_ref, inner_ref, chain, s)
            a, b = halves(jnp.concatenate(parts, axis=0).T)
            high[natural, s] = a
            low[natural, s] = b


def adjugate_4(a):
    def minor(i, j, m, n):
        return a[i][m] * a[j][n] - a[j][m] * a[i][n]

    pairs = [(0, 1), (0, 2), (0, 3), (1, 2), (1, 3), (2, 3)]
    s = [minor(0, 1, m, n) for m, n in pairs]
    c = [minor(2, 3, m, n) for m, n in pairs]
    det = (s[0] * c[5] - s[1] * c[4]) + (s[2] * c[3] + s[3] * c[2]) - (s[4] * c[1] - s[5] * c[0])
    b = [[None] * 4 for _ in range(4)]
    b[0][0] = a[1][1] * c[5] - a[1][2] * c[4] + a[1][3] * c[3]
    b[0][1] = a[0][2] * c[4] - a[0][1] * c[5] - a[0][3] * c[3]
    b[0][2] = a[3][1] * s[5] - a[3][2] * s[4] + a[3][3] * s[3]
    b[0][3] = a[2][2] * s[4] - a[2][1] * s[5] - a[2][3] * s[3]
    b[1][1] = a[0][0] * c[5] - a[0][2] * c[2] + a[0][3] * c[1]
    b[1][2] = a[3][2] * s[2] - a[3][0] * s[5] - a[3][3] * s[1]
    b[1][3] = a[2][0] * s[5] - a[2][2] * s[2] + a[2][3] * s[1]
    b[2][2] = a[3][0] * s[4] - a[3][1] * s[2] + a[3][3] * s[0]
    b[2][3] = a[2][1] * s[2] - a[2][0] * s[4] - a[2][3] * s[0]
    b[3][3] = a[2][0] * s[3] - a[2][1] * s[1] + a[2][2] * s[0]
    for i in range(4):
        for j in range(i):
            b[i][j] = b[j][i]
    return b, det


def lower_inverse_small(a):
    size = len(a)
    low = [[None] * size for _ in range(size)]
    scale = [None] * size
    for j in range(size):
        d = a[j][j]
        for k in range(j):
            d = d - low[j][k] * low[j][k]
        scale[j] = lax.rsqrt(d)
        for i in range(j + 1, size):
            v = a[i][j]
            for k in range(j):
                v = v - low[i][k] * low[j][k]
            low[i][j] = v * scale[j]
    inv = [[None] * size for _ in range(size)]
    for i in range(size):
        inv[i][i] = scale[i]
        for j in range(i):
            v = low[i][j] * inv[j][j]
            for k in range(j + 1, i):
                v = v + low[i][k] * inv[k][j]
            inv[i][j] = -(v * scale[i])
    return inv


def spread_lane(value, lane):
    return jnp.take_along_axis(
        value, jnp.full(value.shape, lane, jnp.int32), axis=1, mode="promise_in_bounds"
    )


def spread_row(value, row):
    return jnp.broadcast_to(value[row : row + 1, :], value.shape)


def lower_inverse(block_ref, out_ref):
    size = block_ref.shape[0]
    shape = (8, size)
    lanes = lax.broadcasted_iota(jnp.int32, shape, 1)
    subs = lax.broadcasted_iota(jnp.int32, shape, 0)
    rows = [block_ref[8 * g : 8 * g + 8, :] for g in range(size // 8)]
    for first in range(0, size, strip):
        past = (first + strip) // 8
        for start in range(first, first + strip, pivots):
            group, offset = divmod(start, 8)
            inside = (lanes >= start) & (lanes < start + pivots)
            here = rows[group]
            columns = {
                g: [spread_lane(rows[g], start + k) for k in range(pivots)]
                for g in range(group, past)
            }
            if start == first:
                corner = [
                    [spread_row(columns[group][j], offset + i) for j in range(pivots)]
                    for i in range(pivots)
                ]
            lines = [
                jnp.where(
                    inside,
                    jnp.where(lanes == start + k, 1.0, 0.0),
                    spread_row(here, offset + k),
                )
                for k in range(pivots)
            ]
            adj, det = adjugate_4(corner)
            share = 1.0 / det
            weights = [
                ((adj[k][0] * lines[0] + adj[k][1] * lines[1]) + (adj[k][2] * lines[2] + adj[k][3] * lines[3]))
                * share
                for k in range(pivots)
            ]
            after = start + pivots
            next_corner = None
            if after < first + strip:
                ng, noff = divmod(after, 8)
                side = [
                    [spread_row(columns[ng][k], noff + i) for k in range(pivots)]
                    for i in range(pivots)
                ]
                ahead = [spread_lane(rows[ng], after + j) for j in range(pivots)]
                part = [
                    [
                        (adj[k][0] * side[j][0] + adj[k][1] * side[j][1])
                        + (adj[k][2] * side[j][2] + adj[k][3] * side[j][3])
                        for j in range(pivots)
                    ]
                    for k in range(pivots)
                ]
                next_corner = [[None] * pivots for _ in range(pivots)]
                for i in range(pivots):
                    for j in range(i + 1):
                        taken = (side[i][0] * part[0][j] + side[i][1] * part[1][j]) + (
                            side[i][2] * part[2][j] + side[i][3] * part[3][j]
                        )
                        next_corner[i][j] = spread_row(ahead[j], noff + i) - taken * share
                        next_corner[j][i] = next_corner[i][j]
            for g in range(group, past):
                c = columns[g]
                change = (c[0] * weights[0] + c[1] * weights[1]) + (c[2] * weights[2] + c[3] * weights[3])
                updated = jnp.where(inside, 0.0, rows[g]) - change
                if g == group:
                    updated = jnp.where(subs >= offset + pivots, updated, rows[g])
                rows[g] = updated
            low = lower_inverse_small(corner)
            for r in range(pivots):
                line = functools.reduce(jnp.add, [low[r][k] * lines[k] for k in range(r + 1)])
                rows[group] = jnp.where(subs == offset + r, line, rows[group])
            corner = next_corner
        mine = (lanes >= first) & (lanes < first + strip)
        for g in range(first // 8, past):
            rows[g] = jnp.where(mine & (lanes > subs + 8 * g), 0.0, rows[g])
            out_ref[8 * g : 8 * g + 8, :] = jnp.where(lanes <= subs + 8 * g, rows[g], 0.0)
        if past < size // 8:
            panel = jnp.concatenate(rows[first // 8 : past], axis=0)
            high, low_part = halves(panel)
            wide = jnp.concatenate([high, low_part, high], axis=0)
            tall = jnp.concatenate([high, high, low_part], axis=0).astype(f32)
            tall = jnp.concatenate([tall, jnp.zeros((-3 * strip % size, size), f32)], axis=0).T
            change = jnp.dot(
                tall[first + strip :, : 3 * strip].astype(bf16), wide, preferred_element_type=f32
            )
            for n, g in enumerate(range(past, size // 8)):
                rows[g] = jnp.where(mine, 0.0, rows[g]) - change[8 * n : 8 * n + 8, :]


def three(left, right):
    a, b = halves(left)
    c, d = halves(right)
    return jnp.dot(
        jnp.concatenate([a, a, b], axis=1),
        jnp.concatenate([c, d, c], axis=0),
        preferred_element_type=f32,
    )


def finish_body(gram_ref, high_ref, low_ref, out_ref, work, diag, lower, panel, inv):
    size = work.shape[0]
    tile = diag.shape[0]
    eye = lax.broadcasted_iota(jnp.int32, (tile, tile), 0) == lax.broadcasted_iota(
        jnp.int32, (tile, tile), 1
    )
    down, across = [], []
    place = -tile
    for i in range(0, size, tile):
        place += i + tile
        kept = jnp.where(eye, gram_ref[place : place + tile, :], 0.0)
        down.append(lax.rsqrt(jnp.sum(kept, axis=1, keepdims=True)))
        across.append(lax.rsqrt(jnp.sum(kept, axis=0, keepdims=True)))
    scales = jnp.concatenate(across, axis=1)
    place = 0
    for i in range(0, size, tile):
        for j in range(0, i + 1, tile):
            block = gram_ref[place : place + tile, :] * down[i // tile] * across[j // tile]
            place += tile
            work[i : i + tile, j : j + tile] = block
            if i != j:
                work[j : j + tile, i : i + tile] = block.T
    cols = lax.broadcasted_iota(jnp.int32, (tile, size), 1)
    local = lax.broadcasted_iota(jnp.int32, (tile, size), 0)

    def outer(b, carry):
        at = pl.multiple_of(b * tile, tile)
        diag[...] = work[pl.ds(at, tile), pl.ds(at, tile)]
        lower_inverse(diag, lower)
        inside = (cols >= at) & (cols < at + tile)
        line = jnp.where(
            inside, jnp.where(cols - at == local, 1.0, 0.0), work[pl.ds(at, tile), :]
        )
        panel[...] = three(lower[...], line)
        kept = jnp.where(cols < at + tile, panel[...] * scales, 0.0)
        high, low = halves(kept)
        inv[pl.ds(at, tile), :size] = high
        inv[pl.ds(at, tile), size:] = low

        def trailing(i, carry):
            to = pl.multiple_of(i * tile, tile)
            change = three(panel[:, pl.ds(to, tile)].T, panel[...])
            work[pl.ds(to, tile), :] = jnp.where(inside, 0.0, work[pl.ds(to, tile), :]) - change
            return carry

        lax.fori_loop(b + 1, size // tile, trailing, 0)
        return carry

    lax.fori_loop(0, size // tile, outer, 0)

    layers, share, orb, _ = out_ref.shape

    def result(s, carry):
        a = jnp.concatenate([high_ref[n, s] for n in range(layers)], axis=0)
        b = jnp.concatenate([low_ref[n, s] for n in range(layers)], axis=0)
        for first in range(0, size, 2 * tile):
            last = first + 2 * tile
            c = inv[first:last, :last]
            d = inv[first:last, size : size + last]
            total = lax.dot_general(
                jnp.concatenate([a[:, :last], a[:, :last], b[:, :last]], axis=1),
                jnp.concatenate([c, d, c], axis=1),
                NT,
                preferred_element_type=f32,
            )
            for n in range(layers):
                out_ref[n, s, :, first:last] = total[n * orb : (n + 1) * orb]
        return carry

    lax.fori_loop(0, share, result, 0)


def group_sum(value, axis_sets):
    if not axis_sets:
        return value
    axes, *rest = axis_sets
    count = lax.axis_size(axes)
    if count == 1:
        return group_sum(value, rest)
    if not rest and count & (count - 1) == 0:
        hop = 1
        while hop < count:
            value = value + lax.ppermute(value, axes, [(i, i ^ hop) for i in range(count)])
            hop *= 2
        return value
    if count > 8 or value.shape[0] % (8 * count):
        return group_sum(lax.psum(value, axes), rest)
    me = lax.axis_index(axes)
    share = value.shape[0] // count

    def piece(k):
        return lax.dynamic_slice_in_dim(value, lax.rem(me + k, count) * share, share, axis=0)

    total = piece(0)
    got = [
        lax.ppermute(piece(k), axes, [(i, (i + k) % count) for i in range(count)])
        for k in range(1, count)
    ]
    for part in got:
        total = total + part
    total = group_sum(total, rest)
    back = [
        lax.ppermute(total, axes, [(i, (i - k) % count) for i in range(count)])
        for k in range(1, count)
    ]
    out = jnp.zeros_like(value)
    out = lax.dynamic_update_slice_in_dim(out, total, me * share, axis=0)
    for k, part in enumerate(back, 1):
        out = lax.dynamic_update_slice_in_dim(out, part, lax.rem(me + k, count) * share, axis=0)
    return out


def per_device(start_states, couplings, potential, site_offsets, coupling_index, degrees):
    layers, sites, orb, count = start_states.shape
    half = count // 2
    total = 2 * layers
    x = lax.axis_index("x").astype(jnp.int32)
    x_arr = x[None]
    depth = lax.axis_size("z")
    states_axes = ("y", "c")
    states = lax.axis_size(states_axes)
    share = sites // states

    def z_move(value, near):
        pairs = []
        for z in range(depth):
            for xx in range(2):
                d = (1 if xx else -1) * (1 if near else -1)
                pairs.append((z * 2 + xx, (z + d) % depth * 2 + xx))
        return lax.ppermute(value, ("z", "x"), pairs)

    with jax.named_scope("prepare"):
        mine_b, other_b, mark = turn_first(x_arr, start_states)
        far = z_move(mine_b, True)
        partner_b = swap(other_b, "x")
        mark = swap(mark, "c")
        lists = call(
            lists_body,
            (x_arr, potential, site_offsets, coupling_index),
            [smem(), vmem(), vmem(), vmem()],
            jax.ShapeDtypeStruct((layers, sites + 16, orb), f32),
            after=(mine_b,),
        )
        their_lists = swap(lists, "x")
        mine_i, other_i = call(
            functools.partial(turn_body, 1),
            (x_arr, start_states),
            [smem(), vmem()],
            [jax.ShapeDtypeStruct((layers - 1, sites, half, orb), f32)] * 2,
            after=(mine_b,),
        )
        table, ends = call(
            table_body,
            (coupling_index.reshape(-1), couplings, potential),
            [smem(), vmem(), vmem()],
            [
                jax.ShapeDtypeStruct((couplings.shape[0], orb, 2 * orb), bf16),
                jax.ShapeDtypeStruct((8, orb), f32),
            ],
            [pltpu.VMEM((couplings.shape[0], 1, orb), f32)] * 2,
            after=(mark,),
        )
        partner_b = hold(partner_b, far, table)
        devices = 2 * depth
        ends = jnp.broadcast_to(ends[None], (devices, *ends.shape))
        ends = jnp.max(lax.all_to_all(ends, ("z", "x"), 0, 0, tiled=True), axis=0)
        near = z_move(partner_b, False)
        partner_i = swap(hold(other_i, partner_b), "x")
        chain = jnp.concatenate([lists, their_lists[::-1]], axis=0)
        pot = chain[:, :sites].reshape(total * sites, orb)
        whole = jnp.swapaxes(chain[:, sites:, :sites], 1, 2).astype(jnp.int32)
        offsets = whole[..., : site_offsets.shape[1]]
        entry = whole[..., 8 : 8 + coupling_index.shape[1]]
        layer_id = jnp.arange(1, total + 1, dtype=jnp.int32)[:, None, None]
        site_id = jnp.arange(sites, dtype=jnp.int32)[None, :, None]
        slots = entry.shape[2]
        one = 1 - 2 * x
        shifts = jnp.where(
            jnp.arange(slots) == slots - 2, -one, jnp.where(jnp.arange(slots) == slots - 1, one, 0)
        ).astype(jnp.int32)
        moved = jnp.concatenate([jnp.zeros_like(offsets[..., :1]), offsets], axis=2)
        source = (layer_id + shifts) * sites + (site_id + moved) % sites
        consts = (source.reshape(-1), entry.reshape(-1), x_arr, table, pot)
        degree = lax.dynamic_slice_in_dim(degrees, x * half, half)
        degree = jnp.broadcast_to(degree[:, None], (half, orb))

    inside = list(range(2, total))

    def sent_after(value):
        mark = call(mark_body, (), [], jax.ShapeDtypeStruct((8, orb), f32), after=(value,))
        return swap(mark, "c")
    group = ("x",) + states_axes

    def regroup(value, axes):
        flat = value.reshape((-1,) + value.shape[2:])
        return lax.all_to_all(flat, axes, 0, 0, tiled=True).reshape(value.shape)

    own_order, their_order = list(range(2, layers + 1)), list(range(layers + 1, total))
    theirs = partner_i[::-1]
    with jax.named_scope("first"):
        four1 = step(
            consts, [partner_b, theirs, far], [[total], their_order, [total + 1]], [total], total,
            after=(ends,),
        )
        near1 = z_move(four1, False)
        one1 = step(consts, [mine_b, mine_i, near], [[1], own_order, [0]], [1], total, after=(four1,))
        far1 = z_move(one1, True)
        in1 = step(
            consts, [mine_b, mine_i, theirs, partner_b], [[1], own_order, their_order, [total]],
            inside, total, after=(one1,),
        )
    start_in = jnp.concatenate([mine_i, theirs], axis=0)
    with jax.named_scope("second"):
        in2, in1s = step(
            consts, [one1, in1, four1], [[1], inside, [total]], inside, total,
            [ends, mine_b, start_in, partner_b], number=2,
        )
        one2, one1s = step(
            consts, [one1, in1, near1], [[1], inside, [0]], [1], total,
            [ends, mine_b, start_in, near], number=2, after=(in2,),
        )
        far2 = z_move(one2, True)
        four2, four1 = step(
            consts, [four1, in1, far1], [[total], inside, [total + 1]], [total], total,
            [ends, partner_b, start_in, far], number=2, after=(sent_after(one2),),
        )
    in1 = in1s
    with jax.named_scope("third"):
        near2 = z_move(four2, False)
        in3_local = step(
            consts, [one2, in2, four2], [[1], inside, [total]], inside, total,
            [ends, in1, degree], (2, states, layers - 1, share, half, orb), number=3,
            after=(sent_after(four2),),
        )
        in3 = regroup(in3_local, group)
        edge_shape = (2, states, 1, share, half, orb)
        four3 = step(
            consts, [four2, in2, far2], [[total], inside, [total + 1]], [total], total,
            [ends, four1, degree], edge_shape, number=3, after=(in3_local,),
        )
        out3_local = step(
            consts, [one2, in2, near2], [[1], inside, [0]], [1], total,
            [ends, one1s, degree], edge_shape, number=3, cost=large, into=four3,
        )
        out3 = regroup(out3_local, group)
    pieces = (out3, in3)
    width = 2 * states * half
    tiles = width // orb
    with jax.named_scope("gram"):
        def gram_of(piece, given, after):
            depth_rows = piece.shape[2] * share * orb
            return call(
                gram_body,
                (piece, *given),
                [vmem()] * (1 + len(given)),
                jax.ShapeDtypeStruct((tiles * (tiles + 1) // 2 * orb, orb), f32),
                [pltpu.VMEM((width, depth_rows), bf16)] * 2,
                after,
            )

        gram = gram_of(in3, (), (sent_after(out3_local),))
        gram = gram_of(out3, (gram,), ())
        high, low = call(
            rows_body,
            (x_arr, *pieces),
            [smem()] + [vmem()] * 2,
            [jax.ShapeDtypeStruct((layers, share, orb, width), bf16)] * 2,
        )
        gram = group_sum(gram, [("c",), ("x", "y"), ("z",)])
    with jax.named_scope("finish"):
        return call(
            finish_body,
            (gram, high, low),
            [vmem()] * 3,
            jax.ShapeDtypeStruct((layers, share, orb, width), f32),
            [
                pltpu.VMEM((width, width), f32),
                pltpu.VMEM((orb, orb), f32),
                pltpu.VMEM((orb, orb), f32),
                pltpu.VMEM((orb, width), f32),
                pltpu.VMEM((width, 2 * width), bf16),
            ],
        )


def solution(mesh):
    blk, states = mesh.shape["blk"], mesh.shape["states"]
    grid = Mesh(
        np.asarray(mesh.devices).reshape(blk // 2, 2, states // 2, 2), ("z", "x", "y", "c")
    )
    b, s = ("z", "x"), ("y", "c")
    in_specs = (
        P(b, None, None, s),
        P(),
        P(b, None, None),
        P(b, None, None),
        P(b, None, None),
        P(s),
    )
    return jax.shard_map(
        per_device, mesh=grid, in_specs=in_specs, out_specs=P(b, s, None, None), check_vma=False
    )
```

```python
import functools

import jax
import jax.numpy as jnp
import numpy as np
from jax import lax
from jax.experimental import pallas as pl
from jax.experimental.pallas import tpu as pltpu
from jax.sharding import Mesh
from jax.sharding import PartitionSpec as P

cut_share = 0.3
exact = lax.Precision.HIGHEST
f32 = jnp.float32
bf16 = jnp.bfloat16
pivots = 4
strip = 64
vmem_limit = 12 * 1024 * 1024
small = pl.CostEstimate(flops=1, bytes_accessed=1, transcendentals=0)
large = pl.CostEstimate(flops=2 * 10**11, bytes_accessed=1, transcendentals=0)
NT = (((1,), (1,)), ((), ()))
TN = (((0,), (0,)), ((), ()))


def vmem():
    return pl.BlockSpec(memory_space=pltpu.VMEM)


def smem():
    return pl.BlockSpec(memory_space=pltpu.SMEM)


def call(body, args, specs, out_shape, scratch=(), after=(), cost=small):
    skipped = len(after)

    def kernel(*refs):
        body(*refs[: len(args)], *refs[len(args) + skipped :])

    return pl.pallas_call(
        kernel,
        out_shape=out_shape,
        in_specs=[*specs, *[pl.BlockSpec(memory_space=pl.ANY)] * skipped],
        out_specs=jax.tree.map(lambda _: vmem(), out_shape),
        scratch_shapes=list(scratch),
        compiler_params=pltpu.CompilerParams(vmem_limit_bytes=vmem_limit),
        cost_estimate=cost,
    )(*args, *after)


def halves(value):
    high = value.astype(bf16)
    return high, (value - high.astype(f32)).astype(bf16)


def hold(value, *after):
    def kernel(*refs):
        pass

    return pl.pallas_call(
        kernel,
        out_shape=jax.ShapeDtypeStruct(value.shape, value.dtype),
        in_specs=[pl.BlockSpec(memory_space=pl.ANY)] * (1 + len(after)),
        out_specs=pl.BlockSpec(memory_space=pl.ANY),
        input_output_aliases={0: 0},
        cost_estimate=small,
    )(value, *after)


def swap(value, axis):
    return lax.ppermute(value, axis, [(0, 1), (1, 0)])


def turn_body(first, x_ref, v_ref, *refs):
    mine, other = refs[-2:]
    layers, sites, _, count = v_ref.shape
    half = count // 2
    x = x_ref[0]
    for j in range(mine.shape[0]):
        layer = x * (layers - 1) + (1 - 2 * x) * (first + j) if layers > 1 else 0

        def one(s, carry):
            turned = v_ref[layer, s].T
            low, high = turned[:half], turned[half:]
            mine[j, s] = jnp.where(x == 0, low, high)
            other[j, s] = jnp.where(x == 0, high, low)
            return carry

        lax.fori_loop(0, sites, one, 0, unroll=16)


def turn_first(x_arr, states):
    layers, sites, orb, count = states.shape

    def kernel(x_ref, v_ref, mine, other, mark):
        turn_body(0, x_ref, v_ref, mine, other)
        mark[...] = jnp.zeros_like(mark)

    shape = (1, sites, count // 2, orb)
    return pl.pallas_call(
        kernel,
        out_shape=[jax.ShapeDtypeStruct(shape, f32)] * 2 + [jax.ShapeDtypeStruct((8, orb), f32)],
        grid_spec=pltpu.PrefetchScalarGridSpec(
            num_scalar_prefetch=1,
            grid=(1,),
            in_specs=[
                pl.BlockSpec((1, sites, orb, count), lambda i, x: (x[0] * (layers - 1), 0, 0, 0))
            ],
            out_specs=[pl.BlockSpec(shape, lambda i, x: (0, 0, 0, 0))] * 2
            + [pl.BlockSpec((8, orb), lambda i, x: (0, 0))],
        ),
        compiler_params=pltpu.CompilerParams(vmem_limit_bytes=vmem_limit),
        cost_estimate=small,
    )(x_arr, states)


def mark_body(out_ref):
    out_ref[...] = jnp.zeros_like(out_ref)


def lists_body(x_ref, pot_ref, offset_ref, entry_ref, out_ref):
    layers, sites, _ = pot_ref.shape
    x = x_ref[0]
    out_ref[...] = jnp.zeros_like(out_ref)
    for j in range(layers):
        layer = x * (layers - 1) + (1 - 2 * x) * j
        out_ref[j, :sites, :] = pot_ref[layer]
        row = sites
        for ref in (offset_ref, entry_ref):
            out_ref[j, row : row + ref.shape[1], :sites] = ref[layer].astype(f32)
            row += 8


def table_body(index_ref, coup_ref, pot_ref, table_ref, ends_ref, row_abs, diag):
    entries, orb, _ = coup_ref.shape
    rows = lax.broadcasted_iota(jnp.int32, (orb, orb), 0)
    cols = lax.broadcasted_iota(jnp.int32, (orb, orb), 1)

    def entry(c, carry):
        turned = coup_ref[c].T
        high, low = halves(turned)
        table_ref[c, :, :orb] = high
        table_ref[c, :, orb:] = low
        row_abs[c] = jnp.sum(jnp.abs(turned), axis=0, keepdims=True)
        diag[c] = jnp.sum(jnp.where(rows == cols, turned, 0.0), axis=0, keepdims=True)
        return carry

    lax.fori_loop(0, entries, entry, 0)
    layers, sites, _ = pot_ref.shape
    slots = index_ref.shape[0] // (layers * sites)

    def block(r, carry):
        top, low = carry
        layer, s = r // sites, lax.rem(r, sites)
        at = layer * slots * sites + s
        own = diag[index_ref[at]]
        center = own + pot_ref[layer, pl.ds(s, 1), :]
        radius = row_abs[index_ref[at]] - jnp.abs(own)
        for k in range(1, slots):
            radius = radius + row_abs[index_ref[at + k * sites]]
        return jnp.maximum(top, center + radius), jnp.maximum(low, radius - center)

    start = jnp.full((1, orb), -jnp.inf, f32)
    top, low = lax.fori_loop(0, layers * sites, block, (start, start))
    ends_ref[...] = jnp.concatenate(
        [jnp.broadcast_to(top, (4, orb)), jnp.broadcast_to(low, (4, orb))], axis=0
    )


def step_body(order, layers_out, total, number, last, *refs):
    refs = list(refs)
    take = lambda count: [refs.pop(0) for _ in range(count)]
    (source_ref, entry_ref, x_ref) = take(3)
    table_ref, pot_ref = take(2)
    pieces = take(len(order))
    ends_ref = take(1)[0] if number > 1 else None
    starts = take(len(order)) if number == 2 else []
    prev = take(1)[0] if number == 3 else None
    degree_ref = take(1)[0] if last else None
    split = refs.pop()
    scaled = refs.pop() if number == 2 else None
    out_ref = refs.pop() if not last else refs[-1]

    lookup, before_of = {}, {}
    for n, chain_layers in enumerate(order):
        for at, layer in enumerate(chain_layers):
            lookup[layer] = (pieces[n], at)
            before_of[layer] = (starts[n], at) if starts else None
    sites, half, orb = pieces[0].shape[1:]
    slots = source_ref.shape[0] // (total * sites)

    if number > 1:
        top = jnp.max(ends_ref[0:1, :], axis=1, keepdims=True)
        low = -jnp.max(ends_ref[4:5, :], axis=1, keepdims=True)
        cut_edge = low + cut_share * (top - low)
        middle = (top + cut_edge) / 2.0
        gain = 1.0 / ((top - cut_edge) / 2.0)

    def field_at(layer, s):
        piece, at = lookup[layer]
        if number != 2:
            return piece[at, s]
        start, at = before_of[layer]
        return (piece[at, s] - middle * start[at, s]) * gain

    for layer in lookup:

        def one(s, carry):
            high, low_part = halves(field_at(layer, s))
            split[layer * sites + s, :half, :] = high
            split[layer * sites + s, half:, :] = low_part
            return carry

        lax.fori_loop(0, sites, one, 0, unroll=16)

    for n, layer in enumerate(layers_out):

        def block(s, carry):
            row = (layer - 1) * sites + s
            left = [split[source_ref[row * slots + k]] for k in range(slots)]
            right = [table_ref[entry_ref[row * slots + k]] for k in range(slots)]
            both = jnp.dot(
                jnp.concatenate(left, axis=1),
                jnp.concatenate(right, axis=0),
                preferred_element_type=f32,
            )
            applied = both[:half, :orb] + (both[:half, orb:] + both[half:, :orb])
            field = field_at(layer, s)
            shift = pot_ref[pl.ds(row, 1), :]
            if number == 1:
                result = applied + shift * field
            else:
                start, start_at = before_of[layer] or (prev, n)
                before = start[start_at, s]
                result = (applied + (shift - middle) * field) * (2.0 * gain) - before
            if number == 2:
                scaled[n, s] = field
            if last:
                degree = degree_ref[...]
                result = jnp.where(degree == 1, before, jnp.where(degree == 2, field, result))
                share = out_ref.shape[3]
                own = layer <= total // 2
                place = max((layer - 1 if own else total - layer) - 1, 0)
                side = (x_ref[0] if own else 1 - x_ref[0]) if out_ref.shape[0] == 2 else 0
                out_ref[side, s // share, place, lax.rem(s, share)] = result
            else:
                out_ref[n, s] = result
            return carry

        lax.fori_loop(0, sites, block, 0, unroll=16)


def step(consts, pieces, order, layers_out, total, more=(), last_shape=None, number=1, after=(), cost=small, into=None):
    sites, half, orb = pieces[0].shape[1:]
    last = last_shape is not None
    shape = last_shape if last else (len(layers_out), sites, half, orb)
    args = [*consts, *pieces, *more]
    scratch = [pltpu.VMEM(((total + 2) * sites, 2 * half, orb), bf16)]
    body = functools.partial(step_body, order, layers_out, total, number, last)
    out = jax.ShapeDtypeStruct(shape, f32)
    one_side = last and len(layers_out) == 1
    if not one_side:
        specs = [smem()] * 3 + [vmem()] * (len(args) - 3)
        return call(body, args, specs, [out, out] if number == 2 else out, scratch, after, cost)
    own = layers_out[0] == 1
    extra = [*after] + ([into] if into is not None else [])
    count = len(args)

    def kernel(*refs):
        body(*refs[:count], *refs[count + len(extra) :])

    zeros = (0,) * (len(shape) - 1)
    return pl.pallas_call(
        kernel,
        out_shape=out,
        grid_spec=pltpu.PrefetchScalarGridSpec(
            num_scalar_prefetch=3,
            grid=(1,),
            in_specs=[vmem()] * (count - 3) + [pl.BlockSpec(memory_space=pl.ANY)] * len(extra),
            out_specs=pl.BlockSpec(
                (1, *shape[1:]), lambda i, a, b, x: (x[0] if own else 1 - x[0], *zeros)
            ),
            scratch_shapes=scratch,
        ),
        input_output_aliases={count + len(after): 0} if into is not None else {},
        compiler_params=pltpu.CompilerParams(vmem_limit_bytes=vmem_limit),
        cost_estimate=cost,
    )(*args, *extra)


def all_states(edge_ref, inner_ref, chain, s):
    ref, layer = (edge_ref, 0) if chain == 0 else (inner_ref, chain - 1)
    return [ref[a, b, layer, s] for b in range(ref.shape[1]) for a in range(2)]


def gram_body(piece_ref, *refs):
    *given, gram_ref, high, low = refs
    _, states, layers, share, half, orb = piece_ref.shape
    col = 0
    for layer in range(layers):
        for s in range(share):
            for n in range(2 * states):
                at = (slice(n * half, (n + 1) * half), slice(col, col + orb))
                high[at], low[at] = halves(piece_ref[n % 2, n // 2, layer, s])
            col += orb
    count = high.shape[0]
    tile = gram_ref.shape[1]
    wide = 2 * tile
    place = 0
    blocks = {}
    for i in range(0, count, wide):
        for j in range(0, i + 1, wide):
            a = [r[i : i + wide, :] for r in (high, high, low, low)]
            b = [r[j : j + wide, :] for r in (high, low, high, low)]
            blocks[i, j] = lax.dot_general(
                jnp.concatenate(a, axis=1),
                jnp.concatenate(b, axis=1),
                NT,
                preferred_element_type=f32,
            )
    for i in range(0, count, tile):
        for j in range(0, i + 1, tile):
            block = blocks[i // wide * wide, j // wide * wide]
            block = block[i % wide : i % wide + tile, j % wide : j % wide + tile]
            for ref in given:
                block = block + ref[place : place + tile, :]
            gram_ref[place : place + tile, :] = block
            place += tile


def rows_body(x_ref, edge_ref, inner_ref, high, low):
    x = x_ref[0]
    layers, share = high.shape[:2]
    for chain in range(layers):
        natural = x * (layers - 1) + (1 - 2 * x) * chain
        for s in range(share):
            parts = all_states(edge_ref, inner_ref, chain, s)
            a, b = halves(jnp.concatenate(parts, axis=0).T)
            high[natural, s] = a
            low[natural, s] = b


def adjugate_4(a):
    def minor(i, j, m, n):
        return a[i][m] * a[j][n] - a[j][m] * a[i][n]

    pairs = [(0, 1), (0, 2), (0, 3), (1, 2), (1, 3), (2, 3)]
    s = [minor(0, 1, m, n) for m, n in pairs]
    c = [minor(2, 3, m, n) for m, n in pairs]
    det = (s[0] * c[5] - s[1] * c[4]) + (s[2] * c[3] + s[3] * c[2]) - (s[4] * c[1] - s[5] * c[0])
    b = [[None] * 4 for _ in range(4)]
    b[0][0] = a[1][1] * c[5] - a[1][2] * c[4] + a[1][3] * c[3]
    b[0][1] = a[0][2] * c[4] - a[0][1] * c[5] - a[0][3] * c[3]
    b[0][2] = a[3][1] * s[5] - a[3][2] * s[4] + a[3][3] * s[3]
    b[0][3] = a[2][2] * s[4] - a[2][1] * s[5] - a[2][3] * s[3]
    b[1][1] = a[0][0] * c[5] - a[0][2] * c[2] + a[0][3] * c[1]
    b[1][2] = a[3][2] * s[2] - a[3][0] * s[5] - a[3][3] * s[1]
    b[1][3] = a[2][0] * s[5] - a[2][2] * s[2] + a[2][3] * s[1]
    b[2][2] = a[3][0] * s[4] - a[3][1] * s[2] + a[3][3] * s[0]
    b[2][3] = a[2][1] * s[2] - a[2][0] * s[4] - a[2][3] * s[0]
    b[3][3] = a[2][0] * s[3] - a[2][1] * s[1] + a[2][2] * s[0]
    for i in range(4):
        for j in range(i):
            b[i][j] = b[j][i]
    return b, det


def lower_inverse_small(a):
    size = len(a)
    low = [[None] * size for _ in range(size)]
    scale = [None] * size
    for j in range(size):
        d = a[j][j]
        for k in range(j):
            d = d - low[j][k] * low[j][k]
        scale[j] = lax.rsqrt(d)
        for i in range(j + 1, size):
            v = a[i][j]
            for k in range(j):
                v = v - low[i][k] * low[j][k]
            low[i][j] = v * scale[j]
    inv = [[None] * size for _ in range(size)]
    for i in range(size):
        inv[i][i] = scale[i]
        for j in range(i):
            v = low[i][j] * inv[j][j]
            for k in range(j + 1, i):
                v = v + low[i][k] * inv[k][j]
            inv[i][j] = -(v * scale[i])
    return inv


def spread_lane(value, lane):
    return jnp.take_along_axis(
        value, jnp.full(value.shape, lane, jnp.int32), axis=1, mode="promise_in_bounds"
    )


def spread_row(value, row):
    return jnp.broadcast_to(value[row : row + 1, :], value.shape)


def lower_inverse(block_ref, out_ref):
    size = block_ref.shape[0]
    shape = (8, size)
    lanes = lax.broadcasted_iota(jnp.int32, shape, 1)
    subs = lax.broadcasted_iota(jnp.int32, shape, 0)
    rows = [block_ref[8 * g : 8 * g + 8, :] for g in range(size // 8)]
    for first in range(0, size, strip):
        past = (first + strip) // 8
        for start in range(first, first + strip, pivots):
            group, offset = divmod(start, 8)
            inside = (lanes >= start) & (lanes < start + pivots)
            here = rows[group]
            columns = {
                g: [spread_lane(rows[g], start + k) for k in range(pivots)]
                for g in range(group, past)
            }
            if start == first:
                corner = [
                    [spread_row(columns[group][j], offset + i) for j in range(pivots)]
                    for i in range(pivots)
                ]
            lines = [
                jnp.where(
                    inside,
                    jnp.where(lanes == start + k, 1.0, 0.0),
                    spread_row(here, offset + k),
                )
                for k in range(pivots)
            ]
            adj, det = adjugate_4(corner)
            share = 1.0 / det
            weights = [
                ((adj[k][0] * lines[0] + adj[k][1] * lines[1]) + (adj[k][2] * lines[2] + adj[k][3] * lines[3]))
                * share
                for k in range(pivots)
            ]
            after = start + pivots
            next_corner = None
            if after < first + strip:
                ng, noff = divmod(after, 8)
                side = [
                    [spread_row(columns[ng][k], noff + i) for k in range(pivots)]
                    for i in range(pivots)
                ]
                ahead = [spread_lane(rows[ng], after + j) for j in range(pivots)]
                part = [
                    [
                        (adj[k][0] * side[j][0] + adj[k][1] * side[j][1])
                        + (adj[k][2] * side[j][2] + adj[k][3] * side[j][3])
                        for j in range(pivots)
                    ]
                    for k in range(pivots)
                ]
                next_corner = [[None] * pivots for _ in range(pivots)]
                for i in range(pivots):
                    for j in range(i + 1):
                        taken = (side[i][0] * part[0][j] + side[i][1] * part[1][j]) + (
                            side[i][2] * part[2][j] + side[i][3] * part[3][j]
                        )
                        next_corner[i][j] = spread_row(ahead[j], noff + i) - taken * share
                        next_corner[j][i] = next_corner[i][j]
            for g in range(group, past):
                c = columns[g]
                change = (c[0] * weights[0] + c[1] * weights[1]) + (c[2] * weights[2] + c[3] * weights[3])
                updated = jnp.where(inside, 0.0, rows[g]) - change
                if g == group:
                    updated = jnp.where(subs >= offset + pivots, updated, rows[g])
                rows[g] = updated
            low = lower_inverse_small(corner)
            for r in range(pivots):
                line = functools.reduce(jnp.add, [low[r][k] * lines[k] for k in range(r + 1)])
                rows[group] = jnp.where(subs == offset + r, line, rows[group])
            corner = next_corner
        mine = (lanes >= first) & (lanes < first + strip)
        for g in range(first // 8, past):
            rows[g] = jnp.where(mine & (lanes > subs + 8 * g), 0.0, rows[g])
            out_ref[8 * g : 8 * g + 8, :] = jnp.where(lanes <= subs + 8 * g, rows[g], 0.0)
        if past < size // 8:
            panel = jnp.concatenate(rows[first // 8 : past], axis=0)
            high, low_part = halves(panel)
            wide = jnp.concatenate([high, low_part, high], axis=0)
            tall = jnp.concatenate([high, high, low_part], axis=0).astype(f32)
            tall = jnp.concatenate([tall, jnp.zeros((-3 * strip % size, size), f32)], axis=0).T
            change = jnp.dot(
                tall[first + strip :, : 3 * strip].astype(bf16), wide, preferred_element_type=f32
            )
            for n, g in enumerate(range(past, size // 8)):
                rows[g] = jnp.where(mine, 0.0, rows[g]) - change[8 * n : 8 * n + 8, :]


def three(left, right):
    a, b = halves(left)
    c, d = halves(right)
    return jnp.dot(
        jnp.concatenate([a, a, b], axis=1),
        jnp.concatenate([c, d, c], axis=0),
        preferred_element_type=f32,
    )


def finish_body(gram_ref, high_ref, low_ref, out_ref, work, diag, lower, panel, inv):
    size = work.shape[0]
    tile = diag.shape[0]
    eye = lax.broadcasted_iota(jnp.int32, (tile, tile), 0) == lax.broadcasted_iota(
        jnp.int32, (tile, tile), 1
    )
    down, across = [], []
    place = -tile
    for i in range(0, size, tile):
        place += i + tile
        kept = jnp.where(eye, gram_ref[place : place + tile, :], 0.0)
        down.append(lax.rsqrt(jnp.sum(kept, axis=1, keepdims=True)))
        across.append(lax.rsqrt(jnp.sum(kept, axis=0, keepdims=True)))
    scales = jnp.concatenate(across, axis=1)
    place = 0
    for i in range(0, size, tile):
        for j in range(0, i + 1, tile):
            block = gram_ref[place : place + tile, :] * down[i // tile] * across[j // tile]
            place += tile
            work[i : i + tile, j : j + tile] = block
            if i != j:
                work[j : j + tile, i : i + tile] = block.T
    cols = lax.broadcasted_iota(jnp.int32, (tile, size), 1)
    local = lax.broadcasted_iota(jnp.int32, (tile, size), 0)

    def outer(b, carry):
        at = pl.multiple_of(b * tile, tile)
        diag[...] = work[pl.ds(at, tile), pl.ds(at, tile)]
        lower_inverse(diag, lower)
        inside = (cols >= at) & (cols < at + tile)
        line = jnp.where(
            inside, jnp.where(cols - at == local, 1.0, 0.0), work[pl.ds(at, tile), :]
        )
        panel[...] = three(lower[...], line)
        kept = jnp.where(cols < at + tile, panel[...] * scales, 0.0)
        high, low = halves(kept)
        inv[pl.ds(at, tile), :size] = high
        inv[pl.ds(at, tile), size:] = low

        def trailing(i, carry):
            to = pl.multiple_of(i * tile, tile)
            change = three(panel[:, pl.ds(to, tile)].T, panel[...])
            work[pl.ds(to, tile), :] = jnp.where(inside, 0.0, work[pl.ds(to, tile), :]) - change
            return carry

        lax.fori_loop(b + 1, size // tile, trailing, 0)
        return carry

    lax.fori_loop(0, size // tile, outer, 0)

    layers, share, orb, _ = out_ref.shape

    def result(s, carry):
        a = jnp.concatenate([high_ref[n, s] for n in range(layers)], axis=0)
        b = jnp.concatenate([low_ref[n, s] for n in range(layers)], axis=0)
        for first in range(0, size, 2 * tile):
            last = first + 2 * tile
            c = inv[first:last, :last]
            d = inv[first:last, size : size + last]
            total = lax.dot_general(
                jnp.concatenate([a[:, :last], a[:, :last], b[:, :last]], axis=1),
                jnp.concatenate([c, d, c], axis=1),
                NT,
                preferred_element_type=f32,
            )
            for n in range(layers):
                out_ref[n, s, :, first:last] = total[n * orb : (n + 1) * orb]
        return carry

    lax.fori_loop(0, share, result, 0)


def group_sum(value, axis_sets):
    if not axis_sets:
        return value
    axes, *rest = axis_sets
    count = lax.axis_size(axes)
    if count == 1:
        return group_sum(value, rest)
    if not rest and count & (count - 1) == 0:
        hop = 1
        while hop < count:
            value = value + lax.ppermute(value, axes, [(i, i ^ hop) for i in range(count)])
            hop *= 2
        return value
    if count > 8 or value.shape[0] % (8 * count):
        return group_sum(lax.psum(value, axes), rest)
    me = lax.axis_index(axes)
    share = value.shape[0] // count

    def piece(k):
        return lax.dynamic_slice_in_dim(value, lax.rem(me + k, count) * share, share, axis=0)

    total = piece(0)
    got = [
        lax.ppermute(piece(k), axes, [(i, (i + k) % count) for i in range(count)])
        for k in range(1, count)
    ]
    for part in got:
        total = total + part
    total = group_sum(total, rest)
    back = [
        lax.ppermute(total, axes, [(i, (i - k) % count) for i in range(count)])
        for k in range(1, count)
    ]
    out = jnp.zeros_like(value)
    out = lax.dynamic_update_slice_in_dim(out, total, me * share, axis=0)
    for k, part in enumerate(back, 1):
        out = lax.dynamic_update_slice_in_dim(out, part, lax.rem(me + k, count) * share, axis=0)
    return out


def per_device(start_states, couplings, potential, site_offsets, coupling_index, degrees):
    layers, sites, orb, count = start_states.shape
    half = count // 2
    total = 2 * layers
    x = lax.axis_index("x").astype(jnp.int32)
    x_arr = x[None]
    depth = lax.axis_size("z")
    states_axes = ("y", "c")
    states = lax.axis_size(states_axes)
    share = sites // states

    def z_move(value, near):
        pairs = []
        for z in range(depth):
            for xx in range(2):
                d = (1 if xx else -1) * (1 if near else -1)
                pairs.append((z * 2 + xx, (z + d) % depth * 2 + xx))
        return lax.ppermute(value, ("z", "x"), pairs)

    with jax.named_scope("prepare"):
        mine_b, other_b, mark = turn_first(x_arr, start_states)
        far = z_move(mine_b, True)
        partner_b = swap(other_b, "x")
        mark = swap(mark, "c")
        lists = call(
            lists_body,
            (x_arr, potential, site_offsets, coupling_index),
            [smem(), vmem(), vmem(), vmem()],
            jax.ShapeDtypeStruct((layers, sites + 16, orb), f32),
            after=(mine_b,),
        )
        their_lists = swap(lists, "x")
        mine_i, other_i = call(
            functools.partial(turn_body, 1),
            (x_arr, start_states),
            [smem(), vmem()],
            [jax.ShapeDtypeStruct((layers - 1, sites, half, orb), f32)] * 2,
            after=(mine_b,),
        )
        table, ends = call(
            table_body,
            (coupling_index.reshape(-1), couplings, potential),
            [smem(), vmem(), vmem()],
            [
                jax.ShapeDtypeStruct((couplings.shape[0], orb, 2 * orb), bf16),
                jax.ShapeDtypeStruct((8, orb), f32),
            ],
            [pltpu.VMEM((couplings.shape[0], 1, orb), f32)] * 2,
            after=(mark,),
        )
        partner_b = hold(partner_b, far, table)
        devices = 2 * depth
        ends = jnp.broadcast_to(ends[None], (devices, *ends.shape))
        ends = jnp.max(lax.all_to_all(ends, ("z", "x"), 0, 0, tiled=True), axis=0)
        near = z_move(partner_b, False)
        partner_i = swap(hold(other_i, partner_b), "x")
        chain = jnp.concatenate([lists, their_lists[::-1]], axis=0)
        pot = chain[:, :sites].reshape(total * sites, orb)
        whole = jnp.swapaxes(chain[:, sites:, :sites], 1, 2).astype(jnp.int32)
        offsets = whole[..., : site_offsets.shape[1]]
        entry = whole[..., 8 : 8 + coupling_index.shape[1]]
        layer_id = jnp.arange(1, total + 1, dtype=jnp.int32)[:, None, None]
        site_id = jnp.arange(sites, dtype=jnp.int32)[None, :, None]
        slots = entry.shape[2]
        one = 1 - 2 * x
        shifts = jnp.where(
            jnp.arange(slots) == slots - 2, -one, jnp.where(jnp.arange(slots) == slots - 1, one, 0)
        ).astype(jnp.int32)
        moved = jnp.concatenate([jnp.zeros_like(offsets[..., :1]), offsets], axis=2)
        source = (layer_id + shifts) * sites + (site_id + moved) % sites
        consts = (source.reshape(-1), entry.reshape(-1), x_arr, table, pot)
        degree = lax.dynamic_slice_in_dim(degrees, x * half, half)
        degree = jnp.broadcast_to(degree[:, None], (half, orb))

    inside = list(range(2, total))

    def sent_after(value):
        mark = call(mark_body, (), [], jax.ShapeDtypeStruct((8, orb), f32), after=(value,))
        return swap(mark, "c")
    group = ("x",) + states_axes

    def regroup(value, axes):
        flat = value.reshape((-1,) + value.shape[2:])
        return lax.all_to_all(flat, axes, 0, 0, tiled=True).reshape(value.shape)

    own_order, their_order = list(range(2, layers + 1)), list(range(layers + 1, total))
    theirs = partner_i[::-1]
    with jax.named_scope("first"):
        four1 = step(
            consts, [partner_b, theirs, far], [[total], their_order, [total + 1]], [total], total,
            after=(ends,),
        )
        near1 = z_move(four1, False)
        one1 = step(consts, [mine_b, mine_i, near], [[1], own_order, [0]], [1], total, after=(four1,))
        far1 = z_move(one1, True)
        in1 = step(
            consts, [mine_b, mine_i, theirs, partner_b], [[1], own_order, their_order, [total]],
            inside, total, after=(one1,),
        )
    start_in = jnp.concatenate([mine_i, theirs], axis=0)
    with jax.named_scope("second"):
        in2, in1s = step(
            consts, [one1, in1, four1], [[1], inside, [total]], inside, total,
            [ends, mine_b, start_in, partner_b], number=2,
        )
        one2, one1s = step(
            consts, [one1, in1, near1], [[1], inside, [0]], [1], total,
            [ends, mine_b, start_in, near], number=2, after=(in2,),
        )
        far2 = z_move(one2, True)
        four2, four1 = step(
            consts, [four1, in1, far1], [[total], inside, [total + 1]], [total], total,
            [ends, partner_b, start_in, far], number=2, after=(sent_after(one2),),
        )
    in1 = in1s
    with jax.named_scope("third"):
        near2 = z_move(four2, False)
        in3_local = step(
            consts, [one2, in2, four2], [[1], inside, [total]], inside, total,
            [ends, in1, degree], (2, states, layers - 1, share, half, orb), number=3,
            after=(sent_after(four2),),
        )
        in3 = regroup(in3_local, group)
        edge_shape = (2, states, 1, share, half, orb)
        four3 = step(
            consts, [four2, in2, far2], [[total], inside, [total + 1]], [total], total,
            [ends, four1, degree], edge_shape, number=3, after=(in3_local,),
        )
        out3_local = step(
            consts, [one2, in2, near2], [[1], inside, [0]], [1], total,
            [ends, one1s, degree], edge_shape, number=3, cost=large, into=four3,
        )
        out3 = regroup(out3_local, group)
    pieces = (out3, in3)
    width = 2 * states * half
    tiles = width // orb
    with jax.named_scope("gram"):
        def gram_of(piece, given, after):
            depth_rows = piece.shape[2] * share * orb
            return call(
                gram_body,
                (piece, *given),
                [vmem()] * (1 + len(given)),
                jax.ShapeDtypeStruct((tiles * (tiles + 1) // 2 * orb, orb), f32),
                [pltpu.VMEM((width, depth_rows), bf16)] * 2,
                after,
            )

        gram = gram_of(in3, (), (sent_after(out3_local),))
        gram = gram_of(out3, (gram,), ())
        high, low = call(
            rows_body,
            (x_arr, *pieces),
            [smem()] + [vmem()] * 2,
            [jax.ShapeDtypeStruct((layers, share, orb, width), bf16)] * 2,
        )
        gram = group_sum(gram, [("c",), ("x", "y"), ("z",)])
    with jax.named_scope("finish"):
        return call(
            finish_body,
            (gram, high, low),
            [vmem()] * 3,
            jax.ShapeDtypeStruct((layers, share, orb, width), f32),
            [
                pltpu.VMEM((width, width), f32),
                pltpu.VMEM((orb, orb), f32),
                pltpu.VMEM((orb, orb), f32),
                pltpu.VMEM((orb, width), f32),
                pltpu.VMEM((width, 2 * width), bf16),
            ],
        )


def solution(mesh):
    blk, states = mesh.shape["blk"], mesh.shape["states"]
    grid = Mesh(
        np.asarray(mesh.devices).reshape(blk // 2, 2, states // 2, 2), ("z", "x", "y", "c")
    )
    b, s = ("z", "x"), ("y", "c")
    in_specs = (
        P(b, None, None, s),
        P(),
        P(b, None, None),
        P(b, None, None),
        P(b, None, None),
        P(s),
    )
    return jax.shard_map(
        per_device, mesh=grid, in_specs=in_specs, out_specs=P(b, s, None, None), check_vma=False
    )
```

```python
import functools

import jax
import jax.numpy as jnp
import numpy as np
from jax import lax
from jax.experimental import pallas as pl
from jax.experimental.pallas import tpu as pltpu
from jax.sharding import Mesh
from jax.sharding import PartitionSpec as P

cut_share = 0.3
exact = lax.Precision.HIGHEST
f32 = jnp.float32
bf16 = jnp.bfloat16
pivots = 4
strip = 64
vmem_limit = 12 * 1024 * 1024
small = pl.CostEstimate(flops=1, bytes_accessed=1, transcendentals=0)
large = pl.CostEstimate(flops=2 * 10**11, bytes_accessed=1, transcendentals=0)
NT = (((1,), (1,)), ((), ()))
TN = (((0,), (0,)), ((), ()))


def vmem():
    return pl.BlockSpec(memory_space=pltpu.VMEM)


def smem():
    return pl.BlockSpec(memory_space=pltpu.SMEM)


def call(body, args, specs, out_shape, scratch=(), after=(), cost=small):
    skipped = len(after)

    def kernel(*refs):
        body(*refs[: len(args)], *refs[len(args) + skipped :])

    return pl.pallas_call(
        kernel,
        out_shape=out_shape,
        in_specs=[*specs, *[pl.BlockSpec(memory_space=pl.ANY)] * skipped],
        out_specs=jax.tree.map(lambda _: vmem(), out_shape),
        scratch_shapes=list(scratch),
        compiler_params=pltpu.CompilerParams(vmem_limit_bytes=vmem_limit),
        cost_estimate=cost,
    )(*args, *after)


def halves(value):
    high = value.astype(bf16)
    return high, (value - high.astype(f32)).astype(bf16)


def hold(value, *after):
    def kernel(*refs):
        pass

    return pl.pallas_call(
        kernel,
        out_shape=jax.ShapeDtypeStruct(value.shape, value.dtype),
        in_specs=[pl.BlockSpec(memory_space=pl.ANY)] * (1 + len(after)),
        out_specs=pl.BlockSpec(memory_space=pl.ANY),
        input_output_aliases={0: 0},
        cost_estimate=small,
    )(value, *after)


def swap(value, axis):
    return lax.ppermute(value, axis, [(0, 1), (1, 0)])


def turn_body(first, x_ref, v_ref, *refs):
    mine, other = refs[-2:]
    layers, sites, _, count = v_ref.shape
    half = count // 2
    x = x_ref[0]
    for j in range(mine.shape[0]):
        layer = x * (layers - 1) + (1 - 2 * x) * (first + j) if layers > 1 else 0

        def one(s, carry):
            turned = v_ref[layer, s].T
            low, high = turned[:half], turned[half:]
            mine[j, s] = jnp.where(x == 0, low, high)
            other[j, s] = jnp.where(x == 0, high, low)
            return carry

        lax.fori_loop(0, sites, one, 0, unroll=16)


def turn_first(x_arr, states):
    layers, sites, orb, count = states.shape

    def kernel(x_ref, v_ref, mine, other, mark):
        turn_body(0, x_ref, v_ref, mine, other)
        mark[...] = jnp.zeros_like(mark)

    shape = (1, sites, count // 2, orb)
    return pl.pallas_call(
        kernel,
        out_shape=[jax.ShapeDtypeStruct(shape, f32)] * 2 + [jax.ShapeDtypeStruct((8, orb), f32)],
        grid_spec=pltpu.PrefetchScalarGridSpec(
            num_scalar_prefetch=1,
            grid=(1,),
            in_specs=[
                pl.BlockSpec((1, sites, orb, count), lambda i, x: (x[0] * (layers - 1), 0, 0, 0))
            ],
            out_specs=[pl.BlockSpec(shape, lambda i, x: (0, 0, 0, 0))] * 2
            + [pl.BlockSpec((8, orb), lambda i, x: (0, 0))],
        ),
        compiler_params=pltpu.CompilerParams(vmem_limit_bytes=vmem_limit),
        cost_estimate=small,
    )(x_arr, states)


def mark_body(out_ref):
    out_ref[...] = jnp.zeros_like(out_ref)


def lists_body(x_ref, pot_ref, offset_ref, entry_ref, out_ref):
    layers, sites, _ = pot_ref.shape
    x = x_ref[0]
    out_ref[...] = jnp.zeros_like(out_ref)
    for j in range(layers):
        layer = x * (layers - 1) + (1 - 2 * x) * j
        out_ref[j, :sites, :] = pot_ref[layer]
        row = sites
        for ref in (offset_ref, entry_ref):
            out_ref[j, row : row + ref.shape[1], :sites] = ref[layer].astype(f32)
            row += 8


def table_body(index_ref, coup_ref, pot_ref, table_ref, ends_ref, row_abs, diag):
    entries, orb, _ = coup_ref.shape
    rows = lax.broadcasted_iota(jnp.int32, (orb, orb), 0)
    cols = lax.broadcasted_iota(jnp.int32, (orb, orb), 1)

    def entry(c, carry):
        turned = coup_ref[c].T
        high, low = halves(turned)
        table_ref[c, :, :orb] = high
        table_ref[c, :, orb:] = low
        row_abs[c] = jnp.sum(jnp.abs(turned), axis=0, keepdims=True)
        diag[c] = jnp.sum(jnp.where(rows == cols, turned, 0.0), axis=0, keepdims=True)
        return carry

    lax.fori_loop(0, entries, entry, 0)
    layers, sites, _ = pot_ref.shape
    slots = index_ref.shape[0] // (layers * sites)

    def block(r, carry):
        top, low = carry
        layer, s = r // sites, lax.rem(r, sites)
        at = layer * slots * sites + s
        own = diag[index_ref[at]]
        center = own + pot_ref[layer, pl.ds(s, 1), :]
        radius = row_abs[index_ref[at]] - jnp.abs(own)
        for k in range(1, slots):
            radius = radius + row_abs[index_ref[at + k * sites]]
        return jnp.maximum(top, center + radius), jnp.maximum(low, radius - center)

    start = jnp.full((1, orb), -jnp.inf, f32)
    top, low = lax.fori_loop(0, layers * sites, block, (start, start))
    ends_ref[...] = jnp.concatenate(
        [jnp.broadcast_to(top, (4, orb)), jnp.broadcast_to(low, (4, orb))], axis=0
    )


def step_body(order, layers_out, total, number, last, *refs):
    refs = list(refs)
    take = lambda count: [refs.pop(0) for _ in range(count)]
    (source_ref, entry_ref, x_ref) = take(3)
    table_ref, pot_ref = take(2)
    pieces = take(len(order))
    ends_ref = take(1)[0] if number > 1 else None
    starts = take(len(order)) if number == 2 else []
    prev = take(1)[0] if number == 3 else None
    degree_ref = take(1)[0] if last else None
    split = refs.pop()
    scaled = refs.pop() if number == 2 else None
    out_ref = refs.pop() if not last else refs[-1]

    lookup, before_of = {}, {}
    for n, chain_layers in enumerate(order):
        for at, layer in enumerate(chain_layers):
            lookup[layer] = (pieces[n], at)
            before_of[layer] = (starts[n], at) if starts else None
    sites, half, orb = pieces[0].shape[1:]
    slots = source_ref.shape[0] // (total * sites)

    if number > 1:
        top = jnp.max(ends_ref[0:1, :], axis=1, keepdims=True)
        low = -jnp.max(ends_ref[4:5, :], axis=1, keepdims=True)
        cut_edge = low + cut_share * (top - low)
        middle = (top + cut_edge) / 2.0
        gain = 1.0 / ((top - cut_edge) / 2.0)

    def field_at(layer, s):
        piece, at = lookup[layer]
        if number != 2:
            return piece[at, s]
        start, at = before_of[layer]
        return (piece[at, s] - middle * start[at, s]) * gain

    for layer in lookup:

        def one(s, carry):
            high, low_part = halves(field_at(layer, s))
            split[layer * sites + s, :half, :] = high
            split[layer * sites + s, half:, :] = low_part
            return carry

        lax.fori_loop(0, sites, one, 0, unroll=16)

    for n, layer in enumerate(layers_out):

        def block(s, carry):
            row = (layer - 1) * sites + s
            left = [split[source_ref[row * slots + k]] for k in range(slots)]
            right = [table_ref[entry_ref[row * slots + k]] for k in range(slots)]
            both = jnp.dot(
                jnp.concatenate(left, axis=1),
                jnp.concatenate(right, axis=0),
                preferred_element_type=f32,
            )
            applied = both[:half, :orb] + (both[:half, orb:] + both[half:, :orb])
            field = field_at(layer, s)
            shift = pot_ref[pl.ds(row, 1), :]
            if number == 1:
                result = applied + shift * field
            else:
                start, start_at = before_of[layer] or (prev, n)
                before = start[start_at, s]
                result = (applied + (shift - middle) * field) * (2.0 * gain) - before
            if number == 2:
                scaled[n, s] = field
            if last:
                degree = degree_ref[...]
                result = jnp.where(degree == 1, before, jnp.where(degree == 2, field, result))
                share = out_ref.shape[3]
                own = layer <= total // 2
                place = max((layer - 1 if own else total - layer) - 1, 0)
                side = (x_ref[0] if own else 1 - x_ref[0]) if out_ref.shape[0] == 2 else 0
                out_ref[side, s // share, place, lax.rem(s, share)] = result
            else:
                out_ref[n, s] = result
            return carry

        lax.fori_loop(0, sites, block, 0, unroll=16)


def step(consts, pieces, order, layers_out, total, more=(), last_shape=None, number=1, after=(), cost=small, into=None):
    sites, half, orb = pieces[0].shape[1:]
    last = last_shape is not None
    shape = last_shape if last else (len(layers_out), sites, half, orb)
    args = [*consts, *pieces, *more]
    scratch = [pltpu.VMEM(((total + 2) * sites, 2 * half, orb), bf16)]
    body = functools.partial(step_body, order, layers_out, total, number, last)
    out = jax.ShapeDtypeStruct(shape, f32)
    one_side = last and len(layers_out) == 1
    if not one_side:
        specs = [smem()] * 3 + [vmem()] * (len(args) - 3)
        return call(body, args, specs, [out, out] if number == 2 else out, scratch, after, cost)
    own = layers_out[0] == 1
    extra = [*after] + ([into] if into is not None else [])
    count = len(args)

    def kernel(*refs):
        body(*refs[:count], *refs[count + len(extra) :])

    zeros = (0,) * (len(shape) - 1)
    return pl.pallas_call(
        kernel,
        out_shape=out,
        grid_spec=pltpu.PrefetchScalarGridSpec(
            num_scalar_prefetch=3,
            grid=(1,),
            in_specs=[vmem()] * (count - 3) + [pl.BlockSpec(memory_space=pl.ANY)] * len(extra),
            out_specs=pl.BlockSpec(
                (1, *shape[1:]), lambda i, a, b, x: (x[0] if own else 1 - x[0], *zeros)
            ),
            scratch_shapes=scratch,
        ),
        input_output_aliases={count + len(after): 0} if into is not None else {},
        compiler_params=pltpu.CompilerParams(vmem_limit_bytes=vmem_limit),
        cost_estimate=cost,
    )(*args, *extra)


def all_states(edge_ref, inner_ref, chain, s):
    ref, layer = (edge_ref, 0) if chain == 0 else (inner_ref, chain - 1)
    return [ref[a, b, layer, s] for b in range(ref.shape[1]) for a in range(2)]


def gram_body(piece_ref, *refs):
    *given, gram_ref, high, low = refs
    _, states, layers, share, half, orb = piece_ref.shape
    col = 0
    for layer in range(layers):
        for s in range(share):
            for n in range(2 * states):
                at = (slice(n * half, (n + 1) * half), slice(col, col + orb))
                high[at], low[at] = halves(piece_ref[n % 2, n // 2, layer, s])
            col += orb
    count = high.shape[0]
    tile = gram_ref.shape[1]
    wide = 2 * tile
    place = 0
    blocks = {}
    for i in range(0, count, wide):
        for j in range(0, i + 1, wide):
            a = [r[i : i + wide, :] for r in (high, high, low, low)]
            b = [r[j : j + wide, :] for r in (high, low, high, low)]
            blocks[i, j] = lax.dot_general(
                jnp.concatenate(a, axis=1),
                jnp.concatenate(b, axis=1),
                NT,
                preferred_element_type=f32,
            )
    for i in range(0, count, tile):
        for j in range(0, i + 1, tile):
            block = blocks[i // wide * wide, j // wide * wide]
            block = block[i % wide : i % wide + tile, j % wide : j % wide + tile]
            for ref in given:
                block = block + ref[place : place + tile, :]
            gram_ref[place : place + tile, :] = block
            place += tile


def rows_body(x_ref, edge_ref, inner_ref, high, low):
    x = x_ref[0]
    layers, share = high.shape[:2]
    for chain in range(layers):
        natural = x * (layers - 1) + (1 - 2 * x) * chain
        for s in range(share):
            parts = all_states(edge_ref, inner_ref, chain, s)
            a, b = halves(jnp.concatenate(parts, axis=0).T)
            high[natural, s] = a
            low[natural, s] = b


def adjugate_4(a):
    def minor(i, j, m, n):
        return a[i][m] * a[j][n] - a[j][m] * a[i][n]

    pairs = [(0, 1), (0, 2), (0, 3), (1, 2), (1, 3), (2, 3)]
    s = [minor(0, 1, m, n) for m, n in pairs]
    c = [minor(2, 3, m, n) for m, n in pairs]
    det = (s[0] * c[5] - s[1] * c[4]) + (s[2] * c[3] + s[3] * c[2]) - (s[4] * c[1] - s[5] * c[0])
    b = [[None] * 4 for _ in range(4)]
    b[0][0] = a[1][1] * c[5] - a[1][2] * c[4] + a[1][3] * c[3]
    b[0][1] = a[0][2] * c[4] - a[0][1] * c[5] - a[0][3] * c[3]
    b[0][2] = a[3][1] * s[5] - a[3][2] * s[4] + a[3][3] * s[3]
    b[0][3] = a[2][2] * s[4] - a[2][1] * s[5] - a[2][3] * s[3]
    b[1][1] = a[0][0] * c[5] - a[0][2] * c[2] + a[0][3] * c[1]
    b[1][2] = a[3][2] * s[2] - a[3][0] * s[5] - a[3][3] * s[1]
    b[1][3] = a[2][0] * s[5] - a[2][2] * s[2] + a[2][3] * s[1]
    b[2][2] = a[3][0] * s[4] - a[3][1] * s[2] + a[3][3] * s[0]
    b[2][3] = a[2][1] * s[2] - a[2][0] * s[4] - a[2][3] * s[0]
    b[3][3] = a[2][0] * s[3] - a[2][1] * s[1] + a[2][2] * s[0]
    for i in range(4):
        for j in range(i):
            b[i][j] = b[j][i]
    return b, det


def lower_inverse_small(a):
    size = len(a)
    low = [[None] * size for _ in range(size)]
    scale = [None] * size
    for j in range(size):
        d = a[j][j]
        for k in range(j):
            d = d - low[j][k] * low[j][k]
        scale[j] = lax.rsqrt(d)
        for i in range(j + 1, size):
            v = a[i][j]
            for k in range(j):
                v = v - low[i][k] * low[j][k]
            low[i][j] = v * scale[j]
    inv = [[None] * size for _ in range(size)]
    for i in range(size):
        inv[i][i] = scale[i]
        for j in range(i):
            v = low[i][j] * inv[j][j]
            for k in range(j + 1, i):
                v = v + low[i][k] * inv[k][j]
            inv[i][j] = -(v * scale[i])
    return inv


def spread_lane(value, lane):
    return jnp.take_along_axis(
        value, jnp.full(value.shape, lane, jnp.int32), axis=1, mode="promise_in_bounds"
    )


def spread_row(value, row):
    return jnp.broadcast_to(value[row : row + 1, :], value.shape)


def lower_inverse(block_ref, out_ref):
    size = block_ref.shape[0]
    shape = (8, size)
    lanes = lax.broadcasted_iota(jnp.int32, shape, 1)
    subs = lax.broadcasted_iota(jnp.int32, shape, 0)
    rows = [block_ref[8 * g : 8 * g + 8, :] for g in range(size // 8)]
    for first in range(0, size, strip):
        past = (first + strip) // 8
        for start in range(first, first + strip, pivots):
            group, offset = divmod(start, 8)
            inside = (lanes >= start) & (lanes < start + pivots)
            here = rows[group]
            columns = {
                g: [spread_lane(rows[g], start + k) for k in range(pivots)]
                for g in range(group, past)
            }
            if start == first:
                corner = [
                    [spread_row(columns[group][j], offset + i) for j in range(pivots)]
                    for i in range(pivots)
                ]
            lines = [
                jnp.where(
                    inside,
                    jnp.where(lanes == start + k, 1.0, 0.0),
                    spread_row(here, offset + k),
                )
                for k in range(pivots)
            ]
            adj, det = adjugate_4(corner)
            share = 1.0 / det
            weights = [
                ((adj[k][0] * lines[0] + adj[k][1] * lines[1]) + (adj[k][2] * lines[2] + adj[k][3] * lines[3]))
                * share
                for k in range(pivots)
            ]
            after = start + pivots
            next_corner = None
            if after < first + strip:
                ng, noff = divmod(after, 8)
                side = [
                    [spread_row(columns[ng][k], noff + i) for k in range(pivots)]
                    for i in range(pivots)
                ]
                ahead = [spread_lane(rows[ng], after + j) for j in range(pivots)]
                part = [
                    [
                        (adj[k][0] * side[j][0] + adj[k][1] * side[j][1])
                        + (adj[k][2] * side[j][2] + adj[k][3] * side[j][3])
                        for j in range(pivots)
                    ]
                    for k in range(pivots)
                ]
                next_corner = [[None] * pivots for _ in range(pivots)]
                for i in range(pivots):
                    for j in range(i + 1):
                        taken = (side[i][0] * part[0][j] + side[i][1] * part[1][j]) + (
                            side[i][2] * part[2][j] + side[i][3] * part[3][j]
                        )
                        next_corner[i][j] = spread_row(ahead[j], noff + i) - taken * share
                        next_corner[j][i] = next_corner[i][j]
            for g in range(group, past):
                c = columns[g]
                change = (c[0] * weights[0] + c[1] * weights[1]) + (c[2] * weights[2] + c[3] * weights[3])
                updated = jnp.where(inside, 0.0, rows[g]) - change
                if g == group:
                    updated = jnp.where(subs >= offset + pivots, updated, rows[g])
                rows[g] = updated
            low = lower_inverse_small(corner)
            for r in range(pivots):
                line = functools.reduce(jnp.add, [low[r][k] * lines[k] for k in range(r + 1)])
                rows[group] = jnp.where(subs == offset + r, line, rows[group])
            corner = next_corner
        mine = (lanes >= first) & (lanes < first + strip)
        for g in range(first // 8, past):
            rows[g] = jnp.where(mine & (lanes > subs + 8 * g), 0.0, rows[g])
            out_ref[8 * g : 8 * g + 8, :] = jnp.where(lanes <= subs + 8 * g, rows[g], 0.0)
        if past < size // 8:
            panel = jnp.concatenate(rows[first // 8 : past], axis=0)
            high, low_part = halves(panel)
            wide = jnp.concatenate([high, low_part, high], axis=0)
            tall = jnp.concatenate([high, high, low_part], axis=0).astype(f32)
            tall = jnp.concatenate([tall, jnp.zeros((-3 * strip % size, size), f32)], axis=0).T
            change = jnp.dot(
                tall[first + strip :, : 3 * strip].astype(bf16), wide, preferred_element_type=f32
            )
            for n, g in enumerate(range(past, size // 8)):
                rows[g] = jnp.where(mine, 0.0, rows[g]) - change[8 * n : 8 * n + 8, :]


def three(left, right):
    a, b = halves(left)
    c, d = halves(right)
    return jnp.dot(
        jnp.concatenate([a, a, b], axis=1),
        jnp.concatenate([c, d, c], axis=0),
        preferred_element_type=f32,
    )


def finish_body(gram_ref, high_ref, low_ref, out_ref, work, diag, lower, panel, inv):
    size = work.shape[0]
    tile = diag.shape[0]
    eye = lax.broadcasted_iota(jnp.int32, (tile, tile), 0) == lax.broadcasted_iota(
        jnp.int32, (tile, tile), 1
    )
    down, across = [], []
    place = -tile
    for i in range(0, size, tile):
        place += i + tile
        kept = jnp.where(eye, gram_ref[place : place + tile, :], 0.0)
        down.append(lax.rsqrt(jnp.sum(kept, axis=1, keepdims=True)))
        across.append(lax.rsqrt(jnp.sum(kept, axis=0, keepdims=True)))
    scales = jnp.concatenate(across, axis=1)
    place = 0
    for i in range(0, size, tile):
        for j in range(0, i + 1, tile):
            block = gram_ref[place : place + tile, :] * down[i // tile] * across[j // tile]
            place += tile
            work[i : i + tile, j : j + tile] = block
            if i != j:
                work[j : j + tile, i : i + tile] = block.T
    cols = lax.broadcasted_iota(jnp.int32, (tile, size), 1)
    local = lax.broadcasted_iota(jnp.int32, (tile, size), 0)

    def outer(b, carry):
        at = pl.multiple_of(b * tile, tile)
        diag[...] = work[pl.ds(at, tile), pl.ds(at, tile)]
        lower_inverse(diag, lower)
        inside = (cols >= at) & (cols < at + tile)
        line = jnp.where(
            inside, jnp.where(cols - at == local, 1.0, 0.0), work[pl.ds(at, tile), :]
        )
        panel[...] = three(lower[...], line)
        kept = jnp.where(cols < at + tile, panel[...] * scales, 0.0)
        high, low = halves(kept)
        inv[pl.ds(at, tile), :size] = high
        inv[pl.ds(at, tile), size:] = low

        def trailing(i, carry):
            to = pl.multiple_of(i * tile, tile)
            change = three(panel[:, pl.ds(to, tile)].T, panel[...])
            work[pl.ds(to, tile), :] = jnp.where(inside, 0.0, work[pl.ds(to, tile), :]) - change
            return carry

        lax.fori_loop(b + 1, size // tile, trailing, 0)
        return carry

    lax.fori_loop(0, size // tile, outer, 0)

    layers, share, orb, _ = out_ref.shape

    def result(s, carry):
        a = jnp.concatenate([high_ref[n, s] for n in range(layers)], axis=0)
        b = jnp.concatenate([low_ref[n, s] for n in range(layers)], axis=0)
        for first in range(0, size, 2 * tile):
            last = first + 2 * tile
            c = inv[first:last, :last]
            d = inv[first:last, size : size + last]
            total = lax.dot_general(
                jnp.concatenate([a[:, :last], a[:, :last], b[:, :last]], axis=1),
                jnp.concatenate([c, d, c], axis=1),
                NT,
                preferred_element_type=f32,
            )
            for n in range(layers):
                out_ref[n, s, :, first:last] = total[n * orb : (n + 1) * orb]
        return carry

    lax.fori_loop(0, share, result, 0)


def group_sum(value, axis_sets):
    if not axis_sets:
        return value
    axes, *rest = axis_sets
    count = lax.axis_size(axes)
    if count == 1:
        return group_sum(value, rest)
    if not rest and count & (count - 1) == 0:
        hop = 1
        while hop < count:
            value = value + lax.ppermute(value, axes, [(i, i ^ hop) for i in range(count)])
            hop *= 2
        return value
    if count > 8 or value.shape[0] % (8 * count):
        return group_sum(lax.psum(value, axes), rest)
    me = lax.axis_index(axes)
    share = value.shape[0] // count

    def piece(k):
        return lax.dynamic_slice_in_dim(value, lax.rem(me + k, count) * share, share, axis=0)

    total = piece(0)
    got = [
        lax.ppermute(piece(k), axes, [(i, (i + k) % count) for i in range(count)])
        for k in range(1, count)
    ]
    for part in got:
        total = total + part
    total = group_sum(total, rest)
    back = [
        lax.ppermute(total, axes, [(i, (i - k) % count) for i in range(count)])
        for k in range(1, count)
    ]
    out = jnp.zeros_like(value)
    out = lax.dynamic_update_slice_in_dim(out, total, me * share, axis=0)
    for k, part in enumerate(back, 1):
        out = lax.dynamic_update_slice_in_dim(out, part, lax.rem(me + k, count) * share, axis=0)
    return out


def per_device(start_states, couplings, potential, site_offsets, coupling_index, degrees):
    layers, sites, orb, count = start_states.shape
    half = count // 2
    total = 2 * layers
    x = lax.axis_index("x").astype(jnp.int32)
    x_arr = x[None]
    depth = lax.axis_size("z")
    states_axes = ("y", "c")
    states = lax.axis_size(states_axes)
    share = sites // states

    def z_move(value, near):
        pairs = []
        for z in range(depth):
            for xx in range(2):
                d = (1 if xx else -1) * (1 if near else -1)
                pairs.append((z * 2 + xx, (z + d) % depth * 2 + xx))
        return lax.ppermute(value, ("z", "x"), pairs)

    with jax.named_scope("prepare"):
        mine_b, other_b, mark = turn_first(x_arr, start_states)
        far = z_move(mine_b, True)
        partner_b = swap(other_b, "x")
        mark = swap(mark, "c")
        lists = call(
            lists_body,
            (x_arr, potential, site_offsets, coupling_index),
            [smem(), vmem(), vmem(), vmem()],
            jax.ShapeDtypeStruct((layers, sites + 16, orb), f32),
            after=(mine_b,),
        )
        their_lists = swap(lists, "x")
        mine_i, other_i = call(
            functools.partial(turn_body, 1),
            (x_arr, start_states),
            [smem(), vmem()],
            [jax.ShapeDtypeStruct((layers - 1, sites, half, orb), f32)] * 2,
            after=(mine_b,),
        )
        table, ends = call(
            table_body,
            (coupling_index.reshape(-1), couplings, potential),
            [smem(), vmem(), vmem()],
            [
                jax.ShapeDtypeStruct((couplings.shape[0], orb, 2 * orb), bf16),
                jax.ShapeDtypeStruct((8, orb), f32),
            ],
            [pltpu.VMEM((couplings.shape[0], 1, orb), f32)] * 2,
            after=(mark,),
        )
        partner_b = hold(partner_b, far, ends)
        devices = 2 * depth
        ends = jnp.broadcast_to(ends[None], (devices, *ends.shape))
        ends = jnp.max(lax.all_to_all(ends, ("z", "x"), 0, 0, tiled=True), axis=0)
        near = z_move(partner_b, False)
        partner_i = swap(hold(other_i, partner_b), "x")
        chain = jnp.concatenate([lists, their_lists[::-1]], axis=0)
        pot = chain[:, :sites].reshape(total * sites, orb)
        whole = jnp.swapaxes(chain[:, sites:, :sites], 1, 2).astype(jnp.int32)
        offsets = whole[..., : site_offsets.shape[1]]
        entry = whole[..., 8 : 8 + coupling_index.shape[1]]
        layer_id = jnp.arange(1, total + 1, dtype=jnp.int32)[:, None, None]
        site_id = jnp.arange(sites, dtype=jnp.int32)[None, :, None]
        slots = entry.shape[2]
        one = 1 - 2 * x
        shifts = jnp.where(
            jnp.arange(slots) == slots - 2, -one, jnp.where(jnp.arange(slots) == slots - 1, one, 0)
        ).astype(jnp.int32)
        moved = jnp.concatenate([jnp.zeros_like(offsets[..., :1]), offsets], axis=2)
        source = (layer_id + shifts) * sites + (site_id + moved) % sites
        consts = (source.reshape(-1), entry.reshape(-1), x_arr, table, pot)
        degree = lax.dynamic_slice_in_dim(degrees, x * half, half)
        degree = jnp.broadcast_to(degree[:, None], (half, orb))

    inside = list(range(2, total))

    def sent_after(value):
        mark = call(mark_body, (), [], jax.ShapeDtypeStruct((8, orb), f32), after=(value,))
        return swap(mark, "c")
    group = ("x",) + states_axes

    def regroup(value, axes):
        flat = value.reshape((-1,) + value.shape[2:])
        return lax.all_to_all(flat, axes, 0, 0, tiled=True).reshape(value.shape)

    own_order, their_order = list(range(2, layers + 1)), list(range(layers + 1, total))
    theirs = partner_i[::-1]
    with jax.named_scope("first"):
        four1 = step(
            consts, [partner_b, theirs, far], [[total], their_order, [total + 1]], [total], total,
            after=(ends,),
        )
        near1 = z_move(four1, False)
        one1 = step(consts, [mine_b, mine_i, near], [[1], own_order, [0]], [1], total, after=(four1,))
        far1 = z_move(one1, True)
        in1 = step(
            consts, [mine_b, mine_i, theirs, partner_b], [[1], own_order, their_order, [total]],
            inside, total, after=(one1,),
        )
    start_in = jnp.concatenate([mine_i, theirs], axis=0)
    with jax.named_scope("second"):
        in2, in1s = step(
            consts, [one1, in1, four1], [[1], inside, [total]], inside, total,
            [ends, mine_b, start_in, partner_b], number=2,
        )
        one2, one1s = step(
            consts, [one1, in1, near1], [[1], inside, [0]], [1], total,
            [ends, mine_b, start_in, near], number=2, after=(in2,),
        )
        far2 = z_move(one2, True)
        four2, four1 = step(
            consts, [four1, in1, far1], [[total], inside, [total + 1]], [total], total,
            [ends, partner_b, start_in, far], number=2, after=(sent_after(one2),),
        )
    in1 = in1s
    with jax.named_scope("third"):
        near2 = z_move(four2, False)
        in3_local = step(
            consts, [one2, in2, four2], [[1], inside, [total]], inside, total,
            [ends, in1, degree], (2, states, layers - 1, share, half, orb), number=3,
            after=(sent_after(four2),),
        )
        in3 = regroup(in3_local, group)
        edge_shape = (2, states, 1, share, half, orb)
        four3 = step(
            consts, [four2, in2, far2], [[total], inside, [total + 1]], [total], total,
            [ends, four1, degree], edge_shape, number=3, after=(in3_local,),
        )
        out3_local = step(
            consts, [one2, in2, near2], [[1], inside, [0]], [1], total,
            [ends, one1s, degree], edge_shape, number=3, cost=large, into=four3,
        )
        out3 = regroup(out3_local, group)
    pieces = (out3, in3)
    width = 2 * states * half
    tiles = width // orb
    with jax.named_scope("gram"):
        def gram_of(piece, given, after):
            depth_rows = piece.shape[2] * share * orb
            return call(
                gram_body,
                (piece, *given),
                [vmem()] * (1 + len(given)),
                jax.ShapeDtypeStruct((tiles * (tiles + 1) // 2 * orb, orb), f32),
                [pltpu.VMEM((width, depth_rows), bf16)] * 2,
                after,
            )

        gram = gram_of(in3, (), (sent_after(out3_local),))
        gram = gram_of(out3, (gram,), ())
        high, low = call(
            rows_body,
            (x_arr, *pieces),
            [smem()] + [vmem()] * 2,
            [jax.ShapeDtypeStruct((layers, share, orb, width), bf16)] * 2,
        )
        gram = group_sum(gram, [("c",), ("x", "y"), ("z",)])
    with jax.named_scope("finish"):
        return call(
            finish_body,
            (gram, high, low),
            [vmem()] * 3,
            jax.ShapeDtypeStruct((layers, share, orb, width), f32),
            [
                pltpu.VMEM((width, width), f32),
                pltpu.VMEM((orb, orb), f32),
                pltpu.VMEM((orb, orb), f32),
                pltpu.VMEM((orb, width), f32),
                pltpu.VMEM((width, 2 * width), bf16),
            ],
        )


def solution(mesh):
    blk, states = mesh.shape["blk"], mesh.shape["states"]
    grid = Mesh(
        np.asarray(mesh.devices).reshape(blk // 2, 2, states // 2, 2), ("z", "x", "y", "c")
    )
    b, s = ("z", "x"), ("y", "c")
    in_specs = (
        P(b, None, None, s),
        P(),
        P(b, None, None),
        P(b, None, None),
        P(b, None, None),
        P(s),
    )
    return jax.shard_map(
        per_device, mesh=grid, in_specs=in_specs, out_specs=P(b, s, None, None), check_vma=False
    )
```
